32 devices in a mesh: fsdp: 8 (over y, x, core), seq: 4 (over z).
Axes of the slice: x: 2, y: 2, z: 4, core: 2. Of those that a mesh axis runs over, the one named last changes fastest.
Arguments:
- tokens: bfloat16 [8, 512, 2048], P('fsdp', 'seq'), may hold values from -13 to 13
- adjacency: int32 [8, 8], replicated, may hold values from 0 to 1, as said below
- w_query: bfloat16 [2048, 1024], P(('fsdp', 'seq')), may hold values from -1 to 1
- w_key: bfloat16 [2048, 256], P(('fsdp', 'seq')), may hold values from -1 to 1
- value_weight: bfloat16 [2048, 256], P(('fsdp', 'seq')), may hold values from -0.125 to 0.125
- grad_attn: bfloat16 [8, 512, 1024], P('fsdp', 'seq'), may hold values from -6 to 6
Outputs:
- attended: bfloat16 [8, 512, 1024], P('fsdp', 'seq')
- grad_tokens: bfloat16 [8, 512, 2048], P('fsdp', 'seq')
- grad_wq: bfloat16 [2048, 1024], P(('fsdp', 'seq'))
- grad_wk: bfloat16 [2048, 256], P(('fsdp', 'seq'))
- grad_wv: bfloat16 [2048, 256], P(('fsdp', 'seq'))
The draws below stay inside these ranges and needn't reach their ends.
Inputs may be any that keep to these rules, and one draw needn't show every extreme that they name: `adjacency`: symmetric, and every diagonal entry is 1.
All inputs are finite; a program needn't handle non-finite values.
Results may differ from the reference program's by a relative error of at most 0.011.
The reference program's roundings to bfloat16 on the way (of `probs_low` and `grad_scores`) count: a program that leaves them out, or rounds other values in their place, can miss the bound.
Values may be sent and summed in bfloat16 or wider, within the bound.
No kernel may reach another device: no remote copies, remote signals or barrier semaphores. Data moves between devices by JAX's collectives and lax.ppermute only.
A program may use at most 128 MiB of HBM per device.

```python
import jax
import jax.numpy as jnp
from jax import lax

MODEL_WIDTH = 2048
HQ = 16
KEY_VALUE_HEADS = 4
HEAD_SIZE = 64
BLK = 64
QUERY_PER_KEY = 4
LEN = 512
SEQS = 8
NB = 8
TOKENS = 4096


def draw_tokens(key, part):
    key = jax.random.fold_in(key, 1)
    key_base = jax.random.fold_in(key, 0)
    result = jnp.clip(jax.random.normal(key_base, (SEQS, LEN, MODEL_WIDTH), jnp.float32), -6.0, 6.0)
    return result.astype(jnp.bfloat16)


def draw_adjacency(key, part):
    key = jax.random.fold_in(key, 2)
    raw = jax.random.randint(key, (NB, NB), 0, 100) < 30
    rows = jnp.arange(NB, dtype=jnp.int32)
    linked = raw | raw.T | (rows[:, None] == rows[None, :])
    return linked.astype(jnp.int32)


def draw_w_query(key, part):
    key = jax.random.fold_in(key, 3)
    weight_bundle = jnp.clip(jax.random.normal(key, (MODEL_WIDTH, HQ * HEAD_SIZE), jnp.float32), -5.0, 5.0) * MODEL_WIDTH ** (-0.5)
    return jnp.clip(weight_bundle, -1.0, 1.0).astype(jnp.bfloat16)


def draw_w_key(key, part):
    key = jax.random.fold_in(key, 4)
    fresh_random = jnp.clip(jax.random.normal(key, (MODEL_WIDTH, KEY_VALUE_HEADS * HEAD_SIZE), jnp.float32), -5.0, 5.0) * MODEL_WIDTH ** (-0.5)
    weight_bundle = fresh_random
    return jnp.clip(weight_bundle, -1.0, 1.0).astype(jnp.bfloat16)


def block_scale(stream_key, dims, shards, smallest, top_value):
    factor_of = 1.0
    for position, parts in shards:
        draws = jax.random.uniform(jax.random.fold_in(jax.random.fold_in(stream_key, 6), position), (parts,), jnp.float32, smallest / len(shards), top_value / len(shards))
        factor_of = factor_of * jnp.repeat(jnp.exp(draws), dims[position] // parts).reshape((-1,) + (1,) * (len(dims) - 1 - position))
    return factor_of


def scatter_about(key, shape, scale, reach, pieces=(), kind=jnp.bfloat16):
    values = jax.random.normal(key, shape, jnp.float32) * scale
    if len(pieces) > 0:
        values = block_scale(key, shape, pieces, -0.22, 0.18) * values
    return jnp.clip(values, min=-reach, max=reach).astype(kind)


def setup_inputs(seed: int = 0) -> dict:
    key_list = jax.random.split(jax.random.key(seed), 7)
    return {
        "tokens": draw_tokens(jax.random.fold_in(key_list[6], 71), 0),
        "adjacency": draw_adjacency(jax.random.fold_in(key_list[6], 71), 0),
        "w_query": draw_w_query(jax.random.fold_in(key_list[6], 71), 0),
        "w_key": draw_w_key(jax.random.fold_in(key_list[6], 71), 0),
        "value_weight": scatter_about(key_list[4], (MODEL_WIDTH, KEY_VALUE_HEADS * HEAD_SIZE), MODEL_WIDTH ** -0.5, 0.125, ((0, 32),)),
        "grad_attn": scatter_about(key_list[5], (SEQS, LEN, HQ * HEAD_SIZE), 1.0, 6.0, ((0, 8), (1, 4))),
    }


def attend_group(query, keys, values, grad_out, allowed):
    scores = jnp.einsum('qhd,kd->hqk', query.astype(jnp.float32), keys.astype(jnp.float32)) * 0.125
    scores = jnp.where(allowed[None], scores, jnp.float32(-1e30))
    highest = jnp.max(scores, axis=-1, keepdims=True)
    expo = jnp.exp(scores - highest)
    probs = expo / jnp.sum(expo, axis=-1, keepdims=True)
    probs_low = probs.astype(jnp.bfloat16)
    output = jnp.einsum('hqk,kd->qhd', probs_low.astype(jnp.float32), values.astype(jnp.float32))
    grad_probs = jnp.einsum('qhd,kd->hqk', grad_out.astype(jnp.float32), values.astype(jnp.float32))
    inner = jnp.sum(probs * grad_probs, axis=-1, keepdims=True)
    grad_scores = (probs * (grad_probs - inner) * 0.125).astype(jnp.bfloat16)
    grad_query = jnp.einsum('hqk,kd->qhd', grad_scores.astype(jnp.float32), keys.astype(jnp.float32))
    grad_keys = jnp.einsum('hqk,qhd->kd', grad_scores.astype(jnp.float32), query.astype(jnp.float32))
    grad_values = jnp.einsum('hqk,qhd->kd', probs_low.astype(jnp.float32), grad_out.astype(jnp.float32))
    return output, grad_query, grad_keys, grad_values


def reference(tokens, adjacency, w_query, w_key, value_weight, grad_attn):
    allowed = jnp.repeat(jnp.repeat(adjacency, BLK, axis=0), BLK, axis=1) > 0
    width_q = HQ * HEAD_SIZE
    key_width = KEY_VALUE_HEADS * HEAD_SIZE

    def one_sequence(carry, inputs):
        seq_tokens, seq_grad = inputs
        query = jnp.dot(seq_tokens, w_query, preferred_element_type=jnp.float32).astype(jnp.bfloat16)
        keys = jnp.dot(seq_tokens, w_key, preferred_element_type=jnp.float32).astype(jnp.bfloat16)
        values = jnp.dot(seq_tokens, value_weight, preferred_element_type=jnp.float32).astype(jnp.bfloat16)
        outs_list, dq_list, dk_list, dv_list = [], [], [], []
        for head_grouping in range(KEY_VALUE_HEADS):
            low = head_grouping * QUERY_PER_KEY * HEAD_SIZE
            high = low + QUERY_PER_KEY * HEAD_SIZE
            group_query = query[:, low:high].reshape(LEN, QUERY_PER_KEY, HEAD_SIZE)
            group_grad = seq_grad[:, low:high].reshape(LEN, QUERY_PER_KEY, HEAD_SIZE)
            group_keys = keys[:, head_grouping * HEAD_SIZE:(head_grouping + 1) * HEAD_SIZE]
            group_values = values[:, head_grouping * HEAD_SIZE:(head_grouping + 1) * HEAD_SIZE]
            output, grad_query, grad_keys, grad_values = attend_group(group_query, group_keys, group_values, group_grad, allowed)
            outs_list.append(output.reshape(LEN, QUERY_PER_KEY * HEAD_SIZE))
            dq_list.append(grad_query.reshape(LEN, QUERY_PER_KEY * HEAD_SIZE))
            dk_list.append(grad_keys)
            dv_list.append(grad_values)
        attended = jnp.concatenate(outs_list, axis=1).astype(jnp.bfloat16)
        grad_query = jnp.concatenate(dq_list, axis=1).astype(jnp.bfloat16)
        grad_keys = jnp.concatenate(dk_list, axis=1).astype(jnp.bfloat16)
        grad_values = jnp.concatenate(dv_list, axis=1).astype(jnp.bfloat16)
        grad_in = jnp.dot(grad_query, w_query.T, preferred_element_type=jnp.float32)
        grad_in = grad_in + jnp.dot(grad_keys, w_key.T, preferred_element_type=jnp.float32)
        grad_in = grad_in + jnp.dot(grad_values, value_weight.T, preferred_element_type=jnp.float32)
        joined = jnp.concatenate([grad_query, grad_keys, grad_values], axis=1)
        carry = carry + jnp.dot(seq_tokens.T, joined, preferred_element_type=jnp.float32)
        return carry, (attended, grad_in.astype(jnp.bfloat16))

    start_sum = jnp.zeros((MODEL_WIDTH, width_q + 2 * key_width), jnp.float32)
    total, (attended, grad_tokens) = lax.scan(one_sequence, start_sum, (tokens, grad_attn))
    total = total * (TOKENS ** -0.5)
    grad_wq = total[:, :width_q].astype(jnp.bfloat16)
    grad_wk = total[:, width_q:width_q + key_width].astype(jnp.bfloat16)
    grad_wv = total[:, width_q + key_width:].astype(jnp.bfloat16)
    return attended, grad_tokens, grad_wq, grad_wk, grad_wv
```

```python
import functools
import math

import jax
import jax.numpy as jnp
from jax import lax
from jax.experimental import pallas as pl
from jax.experimental.pallas import tpu as pltpu
from jax.sharding import PartitionSpec as P

KEY_VALUE_HEADS = 4
HEAD_SIZE = 64
BLK = 64
F32 = jnp.float32
BF16 = jnp.bfloat16
VMEM_LIMIT = 48 * 1024 * 1024


def attend_group(query, keys, values, grad_out, allowed):
    scores = jnp.einsum("qhd,kd->hqk", query, keys, preferred_element_type=F32) * 0.125
    scores = jnp.where(allowed[None], scores, jnp.float32(-1e30))
    highest = jnp.max(scores, axis=-1, keepdims=True)
    expo = jnp.exp(scores - highest)
    probs = expo / jnp.sum(expo, axis=-1, keepdims=True)
    probs_low = probs.astype(BF16)
    output = jnp.einsum("hqk,kd->qhd", probs_low, values, preferred_element_type=F32)
    grad_probs = jnp.einsum("qhd,kd->hqk", grad_out, values, preferred_element_type=F32)
    inner = jnp.sum(probs * grad_probs, axis=-1, keepdims=True)
    grad_scores = (probs * (grad_probs - inner) * 0.125).astype(BF16)
    grad_query = jnp.einsum("hqk,kd->qhd", grad_scores, keys, preferred_element_type=F32)
    grad_keys = jnp.einsum("hqk,qhd->kd", grad_scores, query, preferred_element_type=F32)
    grad_values = jnp.einsum("hqk,qhd->kd", probs_low, grad_out, preferred_element_type=F32)
    return (output, grad_query, grad_keys, grad_values)


def general_body(tokens, adjacency, w_query, w_key, value_weight, grad_attn):
    local_tokens = tokens[0]
    local_grad = grad_attn[0]
    rows_here = local_tokens.shape[0]
    full_q, full_k, full_v = (
        lax.all_gather(w_query, ("fsdp", "seq"), axis=0, tiled=True),
        lax.all_gather(w_key, ("fsdp", "seq"), axis=0, tiled=True),
        lax.all_gather(value_weight, ("fsdp", "seq"), axis=0, tiled=True),
    )
    query = jnp.dot(local_tokens, full_q, preferred_element_type=F32).astype(BF16)
    keys = jnp.dot(local_tokens, full_k, preferred_element_type=F32).astype(BF16)
    values = jnp.dot(local_tokens, full_v, preferred_element_type=F32).astype(BF16)
    all_keys, all_values = (
        lax.all_gather(keys, "seq", axis=0, tiled=True),
        lax.all_gather(values, "seq", axis=0, tiled=True),
    )
    blocks_here = rows_here // BLK
    position = lax.axis_index("seq")
    mask_rows = lax.dynamic_slice_in_dim(adjacency, position * blocks_here, blocks_here, 0)
    allowed = jnp.repeat(jnp.repeat(mask_rows, BLK, axis=0), BLK, axis=1) > 0
    group_size = w_query.shape[1] // w_key.shape[1]
    outs_list, dq_list, dk_list, dv_list = ([], [], [], [])
    for head_grouping in range(KEY_VALUE_HEADS):
        low = head_grouping * group_size * HEAD_SIZE
        high = low + group_size * HEAD_SIZE
        group_query = query[:, low:high].reshape(rows_here, group_size, HEAD_SIZE)
        group_grad = local_grad[:, low:high].reshape(rows_here, group_size, HEAD_SIZE)
        group_keys = all_keys[:, head_grouping * HEAD_SIZE : (head_grouping + 1) * HEAD_SIZE]
        group_values = all_values[:, head_grouping * HEAD_SIZE : (head_grouping + 1) * HEAD_SIZE]
        output, grad_query, grad_keys, grad_values = attend_group(
            group_query, group_keys, group_values, group_grad, allowed
        )
        outs_list.append(output.reshape(rows_here, group_size * HEAD_SIZE))
        dq_list.append(grad_query.reshape(rows_here, group_size * HEAD_SIZE))
        dk_list.append(grad_keys)
        dv_list.append(grad_values)
    attended = jnp.concatenate(outs_list, axis=1).astype(BF16)
    grad_query = jnp.concatenate(dq_list, axis=1).astype(BF16)
    key_terms = jnp.concatenate(dk_list, axis=1)
    value_terms = jnp.concatenate(dv_list, axis=1)
    summed_keys, summed_values = (
        lax.psum_scatter(key_terms, "seq", scatter_dimension=0, tiled=True),
        lax.psum_scatter(value_terms, "seq", scatter_dimension=0, tiled=True),
    )
    grad_keys = summed_keys.astype(BF16)
    grad_values = summed_values.astype(BF16)
    grad_in = jnp.dot(grad_query, full_q.T, preferred_element_type=F32)
    grad_in = grad_in + jnp.dot(grad_keys, full_k.T, preferred_element_type=F32)
    grad_in = grad_in + jnp.dot(grad_values, full_v.T, preferred_element_type=F32)
    joined = jnp.concatenate([grad_query, grad_keys, grad_values], axis=1)
    total_tokens = all_keys.shape[0] * lax.axis_size("fsdp")
    factor = 1.0 / math.sqrt(total_tokens)
    summed = lax.psum_scatter(
        jnp.dot(local_tokens.T, joined, preferred_element_type=F32) * factor,
        ("fsdp", "seq"),
        scatter_dimension=0,
        tiled=True,
    )
    width_q = w_query.shape[1]
    key_width = w_key.shape[1]
    grad_wq = summed[:, :width_q].astype(BF16)
    grad_wk = summed[:, width_q : width_q + key_width].astype(BF16)
    grad_wv = summed[:, width_q + key_width :].astype(BF16)
    return (attended[None], grad_in.astype(BF16)[None], grad_wq, grad_wk, grad_wv)


def swap(x, axis, j):
    n = lax.axis_size(axis)
    return lax.ppermute(x, axis, [(i, i ^ j) for i in range(n)])


def vmem_call(kernel, out_shape, scratch_shapes=(), smem=0, total=0):
    def call(*args):
        in_specs = [
            pl.BlockSpec(memory_space=pltpu.SMEM if i < smem else pltpu.VMEM)
            for i in range(len(args))
        ]
        outs = jax.tree.map(lambda _: pl.BlockSpec(memory_space=pltpu.VMEM), out_shape)
        return pl.pallas_call(
            kernel,
            out_shape=out_shape,
            in_specs=in_specs,
            out_specs=outs,
            scratch_shapes=scratch_shapes,
            compiler_params=pltpu.CompilerParams(vmem_limit_bytes=VMEM_LIMIT),
            cost_estimate=pl.CostEstimate(flops=total, bytes_accessed=4 << 20, transcendentals=0),
        )(*args)

    return call


def shape(*dims, dtype=BF16):
    return jax.ShapeDtypeStruct(dims, dtype)


def group_columns(ref, group, width):
    if width % 128 == 0:
        return ref[:, pl.ds(pl.multiple_of(group * width, width), width)]
    per = 128 // width
    wide = ref[:, pl.ds(pl.multiple_of((group // per) * 128, 128), 128)]
    part = wide[:, :width]
    for i in range(1, per):
        part = jnp.where(group % per == i, wide[:, i * width : (i + 1) * width], part)
    return part


def pack_kernel(place_ref, wq_ref, wk_ref, wv_ref, grad_ref, *outs):
    s = place_ref[1]
    w_all, w_outs, g_outs = outs[0], outs[1:4], outs[4:8]
    wide = wq_ref.shape[1] // 4
    narrow = wk_ref.shape[1] // 4
    for j in range(4):
        g = s ^ j
        q = group_columns(wq_ref, g, wide)
        k = group_columns(wk_ref, g, narrow)
        v = group_columns(wv_ref, g, narrow)
        row = jnp.concatenate([q, k, v], axis=1)
        w_all[j] = row
        if j > 0:
            w_outs[j - 1][...] = row
        g_outs[j][...] = group_columns(grad_ref, g, wide)


def attend_kernel(place_ref, adjacency_ref, *refs):
    f, s = place_ref[0], place_ref[1]
    x_refs, w_refs, g_refs = refs[0:4], refs[4:12], refs[12:16]
    att_refs, d_refs = refs[16:20], refs[20:24]
    w_scr, q_scr, gt_scr = refs[24:27]
    rows = x_refs[0].shape[0]
    length = 4 * rows
    depth = w_refs[0].shape[1]
    span = 4 * depth
    hs = HEAD_SIZE
    per = g_refs[0].shape[1] // hs
    wide = per * hs

    acc = None
    for jf in range(8):
        for l in range(4):
            w_scr[jf, pl.ds(pl.multiple_of((s ^ l) * depth, depth), depth), :] = w_refs[jf][l]
    for jf in range(8):
        cols = pl.ds(pl.multiple_of((f ^ jf) * span, span), span)
        x = jnp.concatenate([r[:, cols] for r in x_refs], axis=0)
        part = jnp.dot(x, w_scr[jf], preferred_element_type=F32)
        acc = part if acc is None else acc + part
    low = acc.astype(BF16)
    q_scr[...] = low[:, :wide]
    keys = low[:, wide : wide + hs]
    values = low[:, wide + hs : wide + 2 * hs]
    keys_t = keys.astype(F32).T.astype(BF16)
    values_t = values.astype(F32).T.astype(BF16)
    for j in range(4):
        gt_scr[j * rows : (j + 1) * rows, :] = g_refs[j][...]

    blocks = length // BLK
    half = rows // BLK

    def absolute(b):
        return (s ^ (b // half)) * half + b % half

    row_block = lax.broadcasted_iota(jnp.int32, (length, 128), 0) // BLK
    lane_block = lax.broadcasted_iota(jnp.int32, (length, 128), 1) // BLK

    tile = 128
    grad_keys = jnp.zeros((length, hs), F32)
    grad_values = jnp.zeros((length, hs), F32)
    out_t = [[None] * per for _ in range(length // tile)]
    dq_t = [[None] * per for _ in range(length // tile)]
    for t in range(length // tile):
        linked = jnp.zeros((length, tile), jnp.int32)
        for b in range(blocks):
            for c in range(tile // BLK):
                a = adjacency_ref[absolute(b), absolute(t * (tile // BLK) + c)]
                linked = jnp.where((row_block == b) & (lane_block == c), a, linked)
        bias = jnp.where(linked > 0, 0.0, -1e30).astype(F32)
        for h in range(per):
            q = q_scr[t * tile : (t + 1) * tile, h * hs : (h + 1) * hs]
            g = gt_scr[t * tile : (t + 1) * tile, h * hs : (h + 1) * hs]
            q8 = (q.astype(F32) * 0.125).astype(BF16)
            last = (((1,), (1,)), ((), ()))
            sc = lax.dot_general(keys, q8, last, preferred_element_type=F32) + bias
            top = jnp.max(sc, axis=0, keepdims=True)
            e = jnp.exp(sc - top)
            p = e * (1.0 / jnp.sum(e, axis=0, keepdims=True))
            p_low = p.astype(BF16)
            dp = lax.dot_general(values, g, last, preferred_element_type=F32)
            inner = jnp.sum(p * dp, axis=0, keepdims=True)
            ds = (p * (dp - inner)).astype(BF16)
            out_t[t][h] = jnp.dot(values_t, p_low, preferred_element_type=F32)
            dq_t[t][h] = jnp.dot(keys_t, ds, preferred_element_type=F32) * 0.125
            grad_keys = grad_keys + jnp.dot(ds, q8, preferred_element_type=F32)
            grad_values = grad_values + jnp.dot(p_low, g, preferred_element_type=F32)
    dkv = jnp.concatenate([grad_keys, grad_values], axis=1).astype(BF16)
    for j in range(4):
        att_refs[j][...] = jnp.concatenate(out_t[j], axis=0).T.astype(BF16)
        dq = jnp.concatenate(dq_t[j], axis=0).T.astype(BF16)
        block = jnp.concatenate([dq, dkv[j * rows : (j + 1) * rows]], axis=1)
        d_refs[j][:rows, :] = block
        d_refs[j ^ 1][rows:, :] = block


def weight_grad_kernel(parity, place_ref, x0, x1, x2, x3, d0_ref, d2_ref, out_ref):
    f, s = place_ref[0], place_ref[1]
    depth = out_ref.shape[2]
    span = 4 * depth
    d = jnp.concatenate([d0_ref[...], d2_ref[...]], axis=0)
    for i in range(4):
        cols = pl.ds(pl.multiple_of((f ^ (2 * i + parity)) * span, span), span)
        x = jnp.concatenate([r[:, cols] for r in (x0, x1, x2, x3)], axis=0)
        part = lax.dot_general(x, d, (((0,), (0,)), ((), ())), preferred_element_type=F32)
        for k in range(4):
            out_ref[i, s ^ k] = part[k * depth : (k + 1) * depth]


def token_grad_kernel(place_ref, d0, d1, d2, d3, *refs):
    f, s = place_ref[0], place_ref[1]
    w_refs, own_ref, send_ref = refs[:8], refs[8], refs[9]
    rows = own_ref.shape[0]
    depth = w_refs[0].shape[2]
    d = [r[...] for r in (d0, d1, d2, d3)]
    last = (((1,), (1,)), ((), ()))
    for jf in range(8):
        halves = []
        for l in range(2):
            total = None
            for j in range(4):
                part = lax.dot_general(
                    d[j], w_refs[jf][l, j ^ (2 * l)], last, preferred_element_type=F32
                )
                total = part if total is None else total + part
            halves.append(total)
        swapped = s // 2 == 1
        first = jnp.where(swapped, halves[1], halves[0])
        second = jnp.where(swapped, halves[0], halves[1])
        both = jnp.concatenate([first, second], axis=1).astype(BF16)
        cols = pl.ds(pl.multiple_of((f ^ jf) * 2 * depth, 2 * depth), 2 * depth)
        own_ref[:, cols] = both[:rows]
        send_ref[:, cols] = both[rows:]


def token_join_kernel(place_ref, own_ref, got_ref, out_ref):
    s = place_ref[1]
    odd = s % 2 == 1
    depth = own_ref.shape[1] // 16
    for b in range(8):
        cols = slice(b * 2 * depth, (b + 1) * 2 * depth)
        own, got = own_ref[:, cols], got_ref[:, cols]
        even = jnp.where(odd, got, own)
        other = jnp.where(odd, own, got)
        out_ref[:, b * 4 * depth : (b + 1) * 4 * depth] = jnp.concatenate(
            [even[:, :depth], other[:, :depth], even[:, depth:], other[:, depth:]], axis=1
        )


def attended_join_kernel(place_ref, a0, a1, a2, a3, out_ref):
    s = place_ref[1]
    wide = a0.shape[1]
    for j, a in enumerate((a0, a1, a2, a3)):
        out_ref[:, pl.ds(pl.multiple_of((s ^ j) * wide, wide), wide)] = a[...]


def weight_join_kernel(place_ref, b0, b1, b2, b3, q_ref, k_ref, v_ref):
    s = place_ref[1]
    wide = q_ref.shape[1] // 4
    narrow = k_ref.shape[1] // 4
    blocks = [b[...] for b in (b0, b1, b2, b3)]
    for j, b in enumerate(blocks):
        q_ref[:, pl.ds(pl.multiple_of((s ^ j) * wide, wide), wide)] = b[:, :wide]
    odd, high = s % 2 == 1, s // 2 == 1
    tails = [b[:, wide:] for b in blocks]
    one = [jnp.where(odd, tails[i ^ 1], tails[i]) for i in range(4)]
    two = [jnp.where(high, one[i ^ 2], one[i]) for i in range(4)]
    k_ref[...] = jnp.concatenate([b[:, :narrow] for b in two], axis=1)
    v_ref[...] = jnp.concatenate([b[:, narrow:] for b in two], axis=1)


def head_body(tokens, adjacency, w_query, w_key, value_weight, grad_attn):
    x0 = tokens[0]
    rows, width = x0.shape
    depth = w_query.shape[0]
    wide = w_query.shape[1] // 4
    narrow = w_key.shape[1] // 4
    joined = wide + 2 * narrow
    place = jnp.stack([lax.axis_index("fsdp"), lax.axis_index("seq")]).astype(jnp.int32)

    x2 = swap(x0, "seq", 2)
    x1 = swap(x0, "seq", 1)
    x3 = swap(x2, "seq", 1)

    packed = vmem_call(
        pack_kernel,
        [shape(4, depth, joined)]
        + [shape(depth, joined)] * 3
        + [shape(rows, wide)] * 4,
        smem=1,
    )(place, w_query, w_key, value_weight, grad_attn[0])
    w_all, w_send, g_send = packed[0], packed[1:4], packed[4:8]

    w_rows = jnp.stack([w_all[0]] + [swap(w_send[j - 1], "seq", j) for j in (1, 2, 3)])
    w_plane = [w_rows] + [swap(w_rows, "fsdp", j) for j in (2, 4, 6)]
    w_other = [swap(w, "fsdp", 1) for w in w_plane]
    w_group = [w_plane[i // 2] if i % 2 == 0 else w_other[i // 2] for i in range(8)]
    g_got = [g_send[0]] + [swap(g_send[j], "seq", j) for j in (1, 2, 3)]

    u_rows = jnp.stack([w_all, swap(w_all, "seq", 2)])
    u_plane = [u_rows] + [swap(u_rows, "fsdp", j) for j in (2, 4, 6)]
    u_other = [swap(u, "fsdp", 1) for u in u_plane]
    u_group = [u_plane[i // 2] if i % 2 == 0 else u_other[i // 2] for i in range(8)]

    results = vmem_call(
        attend_kernel,
        [shape(rows, wide)] * 4 + [shape(2 * rows, joined)] * 4,
        scratch_shapes=[
            pltpu.VMEM((8, 4 * depth, joined), BF16),
            pltpu.VMEM((4 * rows, wide), BF16),
            pltpu.VMEM((4 * rows, wide), BF16),
        ],
        smem=2,
        total=8 << 30,
    )(place, adjacency, x0, x1, x2, x3, *w_group, *g_got)
    att, d = results[:4], results[4:]

    d_got = [d[0]] + [swap(d[j], "seq", j) for j in (1, 2, 3)]

    def weight_grad(parity):
        return vmem_call(
            functools.partial(weight_grad_kernel, parity),
            shape(4, 4, depth, joined, dtype=F32),
            smem=1,
            total=1 << 30,
        )(place, x0, x1, x2, x3, d[0], d[2])

    sent = swap(weight_grad(1), "fsdp", 1)
    kept = weight_grad(0)
    total = [kept[i] + sent[i] for i in range(4)]
    got = [swap(total[i], "fsdp", 2 * i) for i in (1, 2, 3)]
    factor = 1.0 / math.sqrt(4 * rows * lax.axis_size("fsdp"))
    summed = (((total[0] + got[0]) + (got[1] + got[2])) * factor).astype(BF16)
    w_final = [summed[0]] + [swap(summed[j], "seq", j) for j in (1, 2, 3)]

    att_got = [att[0]] + [swap(att[j], "seq", j) for j in (1, 2, 3)]

    own, send = vmem_call(
        token_grad_kernel,
        [shape(rows, width // 2)] * 2,
        smem=1,
        total=1 << 30,
    )(place, *d_got, *u_group)
    half = swap(send, "seq", 1)

    attended = vmem_call(attended_join_kernel, shape(rows, 4 * wide), smem=1)(place, *att_got)
    grad_in = vmem_call(token_join_kernel, shape(rows, width), smem=1)(place, own, half)
    grad_wq, grad_wk, grad_wv = vmem_call(
        weight_join_kernel,
        [shape(depth, 4 * wide), shape(depth, 4 * narrow), shape(depth, 4 * narrow)],
        smem=1,
    )(place, *w_final)
    return attended[None], grad_in[None], grad_wq, grad_wk, grad_wv


def solution(mesh):
    by_heads = mesh.shape["seq"] == KEY_VALUE_HEADS and mesh.shape["fsdp"] == 8
    return jax.shard_map(
        head_body if by_heads else general_body,
        mesh=mesh,
        in_specs=(
            P("fsdp", "seq", None),
            P(),
            P(("fsdp", "seq"), None),
            P(("fsdp", "seq"), None),
            P(("fsdp", "seq"), None),
            P("fsdp", "seq", None),
        ),
        out_specs=(
            P("fsdp", "seq", None),
            P("fsdp", "seq", None),
            P(("fsdp", "seq"), None),
            P(("fsdp", "seq"), None),
            P(("fsdp", "seq"), None),
        ),
        check_vma=False,
    )
```

```python
import functools
import math

import jax
import jax.numpy as jnp
from jax import lax
from jax.experimental import pallas as pl
from jax.experimental.pallas import tpu as pltpu
from jax.sharding import PartitionSpec as P

KEY_VALUE_HEADS = 4
HEAD_SIZE = 64
BLK = 64
F32 = jnp.float32
BF16 = jnp.bfloat16
VMEM_LIMIT = 48 * 1024 * 1024
COST = 2


def attend_group(query, keys, values, grad_out, allowed):
    scores = jnp.einsum("qhd,kd->hqk", query, keys, preferred_element_type=F32) * 0.125
    scores = jnp.where(allowed[None], scores, jnp.float32(-1e30))
    highest = jnp.max(scores, axis=-1, keepdims=True)
    expo = jnp.exp(scores - highest)
    probs = expo / jnp.sum(expo, axis=-1, keepdims=True)
    probs_low = probs.astype(BF16)
    output = jnp.einsum("hqk,kd->qhd", probs_low, values, preferred_element_type=F32)
    grad_probs = jnp.einsum("qhd,kd->hqk", grad_out, values, preferred_element_type=F32)
    inner = jnp.sum(probs * grad_probs, axis=-1, keepdims=True)
    grad_scores = (probs * (grad_probs - inner) * 0.125).astype(BF16)
    grad_query = jnp.einsum("hqk,kd->qhd", grad_scores, keys, preferred_element_type=F32)
    grad_keys = jnp.einsum("hqk,qhd->kd", grad_scores, query, preferred_element_type=F32)
    grad_values = jnp.einsum("hqk,qhd->kd", probs_low, grad_out, preferred_element_type=F32)
    return (output, grad_query, grad_keys, grad_values)


def general_body(tokens, adjacency, w_query, w_key, value_weight, grad_attn):
    local_tokens = tokens[0]
    local_grad = grad_attn[0]
    rows_here = local_tokens.shape[0]
    full_q, full_k, full_v = (
        lax.all_gather(w_query, ("fsdp", "seq"), axis=0, tiled=True),
        lax.all_gather(w_key, ("fsdp", "seq"), axis=0, tiled=True),
        lax.all_gather(value_weight, ("fsdp", "seq"), axis=0, tiled=True),
    )
    query = jnp.dot(local_tokens, full_q, preferred_element_type=F32).astype(BF16)
    keys = jnp.dot(local_tokens, full_k, preferred_element_type=F32).astype(BF16)
    values = jnp.dot(local_tokens, full_v, preferred_element_type=F32).astype(BF16)
    all_keys, all_values = (
        lax.all_gather(keys, "seq", axis=0, tiled=True),
        lax.all_gather(values, "seq", axis=0, tiled=True),
    )
    blocks_here = rows_here // BLK
    position = lax.axis_index("seq")
    mask_rows = lax.dynamic_slice_in_dim(adjacency, position * blocks_here, blocks_here, 0)
    allowed = jnp.repeat(jnp.repeat(mask_rows, BLK, axis=0), BLK, axis=1) > 0
    group_size = w_query.shape[1] // w_key.shape[1]
    outs_list, dq_list, dk_list, dv_list = ([], [], [], [])
    for head_grouping in range(KEY_VALUE_HEADS):
        low = head_grouping * group_size * HEAD_SIZE
        high = low + group_size * HEAD_SIZE
        group_query = query[:, low:high].reshape(rows_here, group_size, HEAD_SIZE)
        group_grad = local_grad[:, low:high].reshape(rows_here, group_size, HEAD_SIZE)
        group_keys = all_keys[:, head_grouping * HEAD_SIZE : (head_grouping + 1) * HEAD_SIZE]
        group_values = all_values[:, head_grouping * HEAD_SIZE : (head_grouping + 1) * HEAD_SIZE]
        output, grad_query, grad_keys, grad_values = attend_group(
            group_query, group_keys, group_values, group_grad, allowed
        )
        outs_list.append(output.reshape(rows_here, group_size * HEAD_SIZE))
        dq_list.append(grad_query.reshape(rows_here, group_size * HEAD_SIZE))
        dk_list.append(grad_keys)
        dv_list.append(grad_values)
    attended = jnp.concatenate(outs_list, axis=1).astype(BF16)
    grad_query = jnp.concatenate(dq_list, axis=1).astype(BF16)
    key_terms = jnp.concatenate(dk_list, axis=1)
    value_terms = jnp.concatenate(dv_list, axis=1)
    summed_keys, summed_values = (
        lax.psum_scatter(key_terms, "seq", scatter_dimension=0, tiled=True),
        lax.psum_scatter(value_terms, "seq", scatter_dimension=0, tiled=True),
    )
    grad_keys = summed_keys.astype(BF16)
    grad_values = summed_values.astype(BF16)
    grad_in = jnp.dot(grad_query, full_q.T, preferred_element_type=F32)
    grad_in = grad_in + jnp.dot(grad_keys, full_k.T, preferred_element_type=F32)
    grad_in = grad_in + jnp.dot(grad_values, full_v.T, preferred_element_type=F32)
    joined = jnp.concatenate([grad_query, grad_keys, grad_values], axis=1)
    total_tokens = all_keys.shape[0] * lax.axis_size("fsdp")
    factor = 1.0 / math.sqrt(total_tokens)
    summed = lax.psum_scatter(
        jnp.dot(local_tokens.T, joined, preferred_element_type=F32) * factor,
        ("fsdp", "seq"),
        scatter_dimension=0,
        tiled=True,
    )
    width_q = w_query.shape[1]
    key_width = w_key.shape[1]
    grad_wq = summed[:, :width_q].astype(BF16)
    grad_wk = summed[:, width_q : width_q + key_width].astype(BF16)
    grad_wv = summed[:, width_q + key_width :].astype(BF16)
    return (attended[None], grad_in.astype(BF16)[None], grad_wq, grad_wk, grad_wv)


def swap(x, axis, j):
    n = lax.axis_size(axis)
    return lax.ppermute(x, axis, [(i, i ^ j) for i in range(n)])


def vmem_call(kernel, out_shape, scratch_shapes=(), smem=0, total=0, place=pltpu.VMEM):
    def call(*args):
        in_specs = [
            pl.BlockSpec(memory_space=pltpu.SMEM if i < smem else place)
            for i in range(len(args))
        ]
        return pl.pallas_call(
            kernel,
            out_shape=out_shape,
            in_specs=in_specs,
            out_specs=jax.tree.map(lambda _: pl.BlockSpec(memory_space=pltpu.VMEM), out_shape),
            scratch_shapes=scratch_shapes,
            compiler_params=pltpu.CompilerParams(vmem_limit_bytes=VMEM_LIMIT),
            cost_estimate=pl.CostEstimate(flops=total, bytes_accessed=4 << 20, transcendentals=0),
        )(*args)

    return call


def shape(*dims, dtype=BF16):
    return jax.ShapeDtypeStruct(dims, dtype)


def group_columns(ref, group, width):
    if width % 128 == 0:
        return ref[:, pl.ds(pl.multiple_of(group * width, width), width)]
    per = 128 // width
    wide = ref[:, pl.ds(pl.multiple_of((group // per) * 128, 128), 128)]
    part = wide[:, :width]
    for i in range(1, per):
        part = jnp.where(group % per == i, wide[:, i * width : (i + 1) * width], part)
    return part


def pack_kernel(place_ref, wq_hbm, wk_hbm, wv_hbm, grad_hbm, w_all, *refs):
    outs, held, sem = refs[:4], refs[4:8], refs[8]
    copies = [
        pltpu.make_async_copy(source, target, sem.at[i])
        for i, (source, target) in enumerate(zip((wq_hbm, wk_hbm, wv_hbm, grad_hbm), held))
    ]
    for copy in copies:
        copy.start()
    for copy in copies:
        copy.wait()
    wq_ref, wk_ref, wv_ref, grad_ref = held
    s = place_ref[1]
    wide = wq_ref.shape[1] // 4
    narrow = wk_ref.shape[1] // 4
    joined = wide + 2 * narrow
    depth = wq_ref.shape[0]
    tail = outs[0].shape[1]
    for j in range(4):
        g = s ^ j
        q = group_columns(wq_ref, g, wide)
        k = group_columns(wk_ref, g, narrow)
        v = group_columns(wv_ref, g, narrow)
        row = jnp.concatenate([q, k, v], axis=1)
        w_all[:, j * joined : (j + 1) * joined] = row
        outs[1][:, tail + j * joined : tail + (j + 1) * joined] = row
        outs[j][:, :joined] = row
        grad = group_columns(grad_ref, g, wide)
        for i in range(grad_ref.shape[0] // depth):
            cols = slice(joined + i * wide, joined + (i + 1) * wide)
            outs[j][:, cols] = grad[i * depth : (i + 1) * depth]


def attend_kernel(place_ref, adjacency_ref, *refs):
    f, s = place_ref[0], place_ref[1]
    x_refs, own_ref, other_ref, pay_refs = refs[0:4], refs[4], refs[5], refs[6:10]
    d_refs = refs[10:14]
    w_scr, q_scr, gt_scr = refs[14:17]
    rows = x_refs[0].shape[0]
    length = 4 * rows
    depth, joined = own_ref.shape[2:]
    span = 4 * depth
    hs = HEAD_SIZE
    wide = joined - 2 * hs
    per = wide // hs

    acc = None
    for jf in range(8):
        w_ref = own_ref if jf % 2 == 0 else other_ref
        for l in range(4):
            place = pl.ds(pl.multiple_of((s ^ l) * depth, depth), depth)
            w_scr[jf, place, :] = w_ref[jf // 2, l]
    for jf in range(8):
        cols = pl.ds(pl.multiple_of((f ^ jf) * span, span), span)
        x = jnp.concatenate([r[:, cols] for r in x_refs], axis=0)
        part = jnp.dot(x, w_scr[jf], preferred_element_type=F32)
        acc = part if acc is None else acc + part
    low = acc.astype(BF16)
    q_scr[...] = low[:, :wide]
    keys = low[:, wide : wide + hs]
    values = low[:, wide + hs : wide + 2 * hs]
    keys_t = keys.astype(F32).T.astype(BF16)
    values_t = values.astype(F32).T.astype(BF16)
    for j in range(4):
        for i in range(rows // depth):
            cols = slice(joined + i * wide, joined + (i + 1) * wide)
            gt_scr[j * rows + i * depth : j * rows + (i + 1) * depth, :] = pay_refs[j][:, cols]

    blocks = length // BLK
    half = rows // BLK

    def absolute(b):
        return (s ^ (b // half)) * half + b % half

    row_block = lax.broadcasted_iota(jnp.int32, (length, 128), 0) // BLK
    lane_block = lax.broadcasted_iota(jnp.int32, (length, 128), 1) // BLK

    tile = 128
    grad_keys = jnp.zeros((length, hs), F32)
    grad_values = jnp.zeros((length, hs), F32)
    out_t = [[None] * per for _ in range(length // tile)]
    dq_t = [[None] * per for _ in range(length // tile)]
    for t in range(length // tile):
        linked = jnp.zeros((length, tile), jnp.int32)
        for b in range(blocks):
            for c in range(tile // BLK):
                a = adjacency_ref[absolute(b), absolute(t * (tile // BLK) + c)]
                linked = jnp.where((row_block == b) & (lane_block == c), a, linked)
        bias = jnp.where(linked > 0, 0.0, -1e30).astype(F32)
        for h in range(per):
            q = q_scr[t * tile : (t + 1) * tile, h * hs : (h + 1) * hs]
            g = gt_scr[t * tile : (t + 1) * tile, h * hs : (h + 1) * hs]
            q8 = (q.astype(F32) * 0.125).astype(BF16)
            last = (((1,), (1,)), ((), ()))
            sc = lax.dot_general(keys, q8, last, preferred_element_type=F32) + bias
            top = jnp.max(sc, axis=0, keepdims=True)
            e = jnp.exp(sc - top)
            p = e * (1.0 / jnp.sum(e, axis=0, keepdims=True))
            p_low = p.astype(BF16)
            dp = lax.dot_general(values, g, last, preferred_element_type=F32)
            inner = jnp.sum(p * dp, axis=0, keepdims=True)
            ds = (p * (dp - inner)).astype(BF16)
            out_t[t][h] = jnp.dot(values_t, p_low, preferred_element_type=F32)
            dq_t[t][h] = jnp.dot(keys_t, ds, preferred_element_type=F32) * 0.125
            grad_keys = grad_keys + jnp.dot(ds, q8, preferred_element_type=F32)
            grad_values = grad_values + jnp.dot(p_low, g, preferred_element_type=F32)
    dkv = jnp.concatenate([grad_keys, grad_values], axis=1).astype(BF16)
    for j in range(4):
        att = jnp.concatenate(out_t[j], axis=0).T.astype(BF16)
        dq = jnp.concatenate(dq_t[j], axis=0).T.astype(BF16)
        block = jnp.concatenate([dq, dkv[j * rows : (j + 1) * rows]], axis=1)
        d_refs[j][:rows, :joined] = block
        d_refs[j ^ 2][rows:, :joined] = block
        d_refs[j][:rows, joined:] = att[:, : wide // 2]
        d_refs[j][rows:, joined:] = att[:, wide // 2 :]


def weight_grad_kernel(parity, place_ref, x0, x1, x2, x3, d0_ref, d1_ref, out_ref):
    f, s = place_ref[0], place_ref[1]
    depth, joined = out_ref.shape[2:]
    span = 4 * depth
    d = jnp.concatenate([d0_ref[:, :joined], d1_ref[:, :joined]], axis=0)
    for i in range(4):
        cols = pl.ds(pl.multiple_of((f ^ (2 * i + parity)) * span, span), span)
        x = jnp.concatenate([r[:, cols] for r in (x0, x2, x1, x3)], axis=0)
        part = lax.dot_general(x, d, (((0,), (0,)), ((), ())), preferred_element_type=F32)
        for k in range(4):
            out_ref[i, s ^ k] = part[k * depth : (k + 1) * depth]


def token_grad_kernel(place_ref, d0, d1, d2, d3, even_ref, odd_ref, own_ref, send_ref):
    f, s = place_ref[0], place_ref[1]
    rows = own_ref.shape[0]
    depth, columns = even_ref.shape[2:]
    joined = columns // 4
    last = (((1,), (1,)), ((), ()))
    sides = []
    for l, order in enumerate(((d0, d1, d2, d3), (d1, d0, d3, d2))):
        d = jnp.concatenate([r[:, :joined] for r in order], axis=1)
        w = jnp.concatenate([(even_ref, odd_ref)[i % 2][i // 2, l] for i in range(8)], axis=0)
        sides.append(lax.dot_general(d, w, last, preferred_element_type=F32).astype(BF16))
    odd = s % 2 == 1
    first = jnp.where(odd, sides[1], sides[0])
    second = jnp.where(odd, sides[0], sides[1])
    for i in range(8):
        part = slice(i * depth, (i + 1) * depth)
        both = jnp.concatenate([first[:, part], second[:, part]], axis=1)
        cols = pl.ds(pl.multiple_of((f ^ i) * 2 * depth, 2 * depth), 2 * depth)
        own_ref[:, cols] = both[:rows]
        send_ref[:, cols] = both[rows:]


def token_join_kernel(place_ref, own_ref, got_ref, out_ref):
    high = place_ref[1] // 2
    part = own_ref.shape[1] // 8
    for i in range(8):
        cols = slice(i * part, (i + 1) * part)
        here = pl.multiple_of((2 * i + high) * part, part)
        there = pl.multiple_of((2 * i + 1 - high) * part, part)
        out_ref[:, pl.ds(here, part)] = own_ref[:, cols]
        out_ref[:, pl.ds(there, part)] = got_ref[:, cols]


def attended_join_kernel(place_ref, d0, d1, d2, d3, out_ref):
    s = place_ref[1]
    rows = out_ref.shape[0]
    part = out_ref.shape[1] // 8
    for j, ref in enumerate((d0, d1, d2, d3)):
        both = jnp.concatenate([ref[:rows, -part:], ref[rows:, -part:]], axis=1)
        out_ref[:, pl.ds(pl.multiple_of((s ^ j) * 2 * part, 2 * part), 2 * part)] = both


def weight_join_kernel(place_ref, b0, b1, b2, b3, q_ref, k_ref, v_ref):
    s = place_ref[1]
    wide = q_ref.shape[1] // 4
    narrow = k_ref.shape[1] // 4
    blocks = [b[...] for b in (b0, b1, b2, b3)]
    for j, b in enumerate(blocks):
        q_ref[:, pl.ds(pl.multiple_of((s ^ j) * wide, wide), wide)] = b[:, :wide]
    odd, high = s % 2 == 1, s // 2 == 1
    tails = [b[:, wide:] for b in blocks]
    one = [jnp.where(odd, tails[i ^ 1], tails[i]) for i in range(4)]
    two = [jnp.where(high, one[i ^ 2], one[i]) for i in range(4)]
    k_ref[...] = jnp.concatenate([b[:, :narrow] for b in two], axis=1)
    v_ref[...] = jnp.concatenate([b[:, narrow:] for b in two], axis=1)


def head_body(tokens, adjacency, w_query, w_key, value_weight, grad_attn):
    x0 = tokens[0]
    rows, width = x0.shape
    depth = w_query.shape[0]
    wide = w_query.shape[1] // 4
    narrow = w_key.shape[1] // 4
    joined = wide + 2 * narrow
    place = jnp.stack([lax.axis_index("fsdp"), lax.axis_index("seq")]).astype(jnp.int32)

    x1 = swap(x0, "seq", 1)
    x2 = swap(x0, "seq", 2)

    few = joined + rows // depth * wide
    w_all, *pay = vmem_call(
        pack_kernel,
        [shape(depth, 4 * joined)]
        + [shape(depth, few + (4 * joined if j == 1 else 0)) for j in range(4)],
        scratch_shapes=[
            pltpu.VMEM((depth, 4 * wide), BF16),
            pltpu.VMEM((depth, 4 * narrow), BF16),
            pltpu.VMEM((depth, 4 * narrow), BF16),
            pltpu.VMEM((rows, 4 * wide), BF16),
            pltpu.SemaphoreType.DMA((4,)),
        ],
        smem=1,
        place=pltpu.HBM,
    )(place, w_query, w_key, value_weight, grad_attn[0])

    pay = [pay[0]] + [swap(pay[j], "seq", j) for j in (1, 2, 3)]
    pay, x1 = lax.optimization_barrier((pay, x1))

    w_rows = jnp.stack([p[:, :joined] for p in pay])
    w_own = jnp.stack([w_rows] + [swap(w_rows, "fsdp", j) for j in (2, 4, 6)])
    u_rows = jnp.stack([w_all, pay[1][:, few:]])
    w_own, x2, u_rows = lax.optimization_barrier((w_own, x2, u_rows))

    x3 = swap(x2, "seq", 1)
    w_other = swap(w_own, "fsdp", 1)
    u_own = jnp.stack([u_rows] + [swap(u_rows, "fsdp", j) for j in (2, 4, 6)])
    u_other = swap(u_own, "fsdp", 1)

    d = vmem_call(
        attend_kernel,
        [shape(2 * rows, joined + wide // 2)] * 4,
        scratch_shapes=[
            pltpu.VMEM((8, 4 * depth, joined), BF16),
            pltpu.VMEM((4 * rows, wide), BF16),
            pltpu.VMEM((4 * rows, wide), BF16),
        ],
        smem=2,
        total=20 << 30,
    )(place, adjacency, x0, x1, x2, x3, w_own, w_other, *pay)

    def weight_grad(parity, d):
        return vmem_call(
            functools.partial(weight_grad_kernel, parity),
            shape(4, 4, depth, joined, dtype=F32),
            smem=1,
            total=1 << 30,
        )(place, x0, x1, x2, x3, d[0], d[1])

    away = weight_grad(1, d)
    d, away = lax.optimization_barrier((d, away))
    sent = swap(away, "fsdp", 1)
    d_got = [d[0]] + [swap(d[j], "seq", j) for j in (1, 2, 3)]
    kept = weight_grad(0, d)
    total = kept + sent
    got = [swap(total[i], "fsdp", 2 * i) for i in (1, 2, 3)]
    factor = 1.0 / math.sqrt(4 * rows * lax.axis_size("fsdp"))
    summed = (((total[0] + got[0]) + (got[1] + got[2])) * factor).astype(BF16)
    w_final = [summed[0]] + [swap(summed[j], "seq", j) for j in (1, 2, 3)]

    own, send = vmem_call(
        token_grad_kernel,
        [shape(rows, width // 2)] * 2,
        smem=1,
        total=COST << 30,
    )(place, *d_got, u_own, u_other)
    half = swap(send, "seq", 2)

    attended = vmem_call(attended_join_kernel, shape(rows, 4 * wide), smem=1)(place, *d_got)
    grad_in = vmem_call(token_join_kernel, shape(rows, width), smem=1)(place, own, half)
    grad_wq, grad_wk, grad_wv = vmem_call(
        weight_join_kernel,
        [shape(depth, 4 * wide), shape(depth, 4 * narrow), shape(depth, 4 * narrow)],
        smem=1,
    )(place, *w_final)
    return attended[None], grad_in[None], grad_wq, grad_wk, grad_wv


def solution(mesh):
    by_heads = mesh.shape["seq"] == KEY_VALUE_HEADS and mesh.shape["fsdp"] == 8
    return jax.shard_map(
        head_body if by_heads else general_body,
        mesh=mesh,
        in_specs=(
            P("fsdp", "seq", None),
            P(),
            P(("fsdp", "seq"), None),
            P(("fsdp", "seq"), None),
            P(("fsdp", "seq"), None),
            P("fsdp", "seq", None),
        ),
        out_specs=(
            P("fsdp", "seq", None),
            P("fsdp", "seq", None),
            P(("fsdp", "seq"), None),
            P(("fsdp", "seq"), None),
            P(("fsdp", "seq"), None),
        ),
        check_vma=False,
    )
```

```python
import functools
import math

import jax
import jax.numpy as jnp
from jax import lax
from jax.experimental import pallas as pl
from jax.experimental.pallas import tpu as pltpu
from jax.sharding import PartitionSpec as P

KEY_VALUE_HEADS = 4
HEAD_SIZE = 64
BLK = 64
F32 = jnp.float32
BF16 = jnp.bfloat16
VMEM_LIMIT = 48 * 1024 * 1024


def attend_group(query, keys, values, grad_out, allowed):
    scores = jnp.einsum("qhd,kd->hqk", query, keys, preferred_element_type=F32) * 0.125
    scores = jnp.where(allowed[None], scores, jnp.float32(-1e30))
    highest = jnp.max(scores, axis=-1, keepdims=True)
    expo = jnp.exp(scores - highest)
    probs = expo / jnp.sum(expo, axis=-1, keepdims=True)
    probs_low = probs.astype(BF16)
    output = jnp.einsum("hqk,kd->qhd", probs_low, values, preferred_element_type=F32)
    grad_probs = jnp.einsum("qhd,kd->hqk", grad_out, values, preferred_element_type=F32)
    inner = jnp.sum(probs * grad_probs, axis=-1, keepdims=True)
    grad_scores = (probs * (grad_probs - inner) * 0.125).astype(BF16)
    grad_query = jnp.einsum("hqk,kd->qhd", grad_scores, keys, preferred_element_type=F32)
    grad_keys = jnp.einsum("hqk,qhd->kd", grad_scores, query, preferred_element_type=F32)
    grad_values = jnp.einsum("hqk,qhd->kd", probs_low, grad_out, preferred_element_type=F32)
    return (output, grad_query, grad_keys, grad_values)


def general_body(tokens, adjacency, w_query, w_key, value_weight, grad_attn):
    local_tokens = tokens[0]
    local_grad = grad_attn[0]
    rows_here = local_tokens.shape[0]
    full_q, full_k, full_v = (
        lax.all_gather(w_query, ("fsdp", "seq"), axis=0, tiled=True),
        lax.all_gather(w_key, ("fsdp", "seq"), axis=0, tiled=True),
        lax.all_gather(value_weight, ("fsdp", "seq"), axis=0, tiled=True),
    )
    query = jnp.dot(local_tokens, full_q, preferred_element_type=F32).astype(BF16)
    keys = jnp.dot(local_tokens, full_k, preferred_element_type=F32).astype(BF16)
    values = jnp.dot(local_tokens, full_v, preferred_element_type=F32).astype(BF16)
    all_keys, all_values = (
        lax.all_gather(keys, "seq", axis=0, tiled=True),
        lax.all_gather(values, "seq", axis=0, tiled=True),
    )
    blocks_here = rows_here // BLK
    position = lax.axis_index("seq")
    mask_rows = lax.dynamic_slice_in_dim(adjacency, position * blocks_here, blocks_here, 0)
    allowed = jnp.repeat(jnp.repeat(mask_rows, BLK, axis=0), BLK, axis=1) > 0
    group_size = w_query.shape[1] // w_key.shape[1]
    outs_list, dq_list, dk_list, dv_list = ([], [], [], [])
    for head_grouping in range(KEY_VALUE_HEADS):
        low = head_grouping * group_size * HEAD_SIZE
        high = low + group_size * HEAD_SIZE
        group_query = query[:, low:high].reshape(rows_here, group_size, HEAD_SIZE)
        group_grad = local_grad[:, low:high].reshape(rows_here, group_size, HEAD_SIZE)
        group_keys = all_keys[:, head_grouping * HEAD_SIZE : (head_grouping + 1) * HEAD_SIZE]
        group_values = all_values[:, head_grouping * HEAD_SIZE : (head_grouping + 1) * HEAD_SIZE]
        output, grad_query, grad_keys, grad_values = attend_group(
            group_query, group_keys, group_values, group_grad, allowed
        )
        outs_list.append(output.reshape(rows_here, group_size * HEAD_SIZE))
        dq_list.append(grad_query.reshape(rows_here, group_size * HEAD_SIZE))
        dk_list.append(grad_keys)
        dv_list.append(grad_values)
    attended = jnp.concatenate(outs_list, axis=1).astype(BF16)
    grad_query = jnp.concatenate(dq_list, axis=1).astype(BF16)
    key_terms = jnp.concatenate(dk_list, axis=1)
    value_terms = jnp.concatenate(dv_list, axis=1)
    summed_keys, summed_values = (
        lax.psum_scatter(key_terms, "seq", scatter_dimension=0, tiled=True),
        lax.psum_scatter(value_terms, "seq", scatter_dimension=0, tiled=True),
    )
    grad_keys = summed_keys.astype(BF16)
    grad_values = summed_values.astype(BF16)
    grad_in = jnp.dot(grad_query, full_q.T, preferred_element_type=F32)
    grad_in = grad_in + jnp.dot(grad_keys, full_k.T, preferred_element_type=F32)
    grad_in = grad_in + jnp.dot(grad_values, full_v.T, preferred_element_type=F32)
    joined = jnp.concatenate([grad_query, grad_keys, grad_values], axis=1)
    total_tokens = all_keys.shape[0] * lax.axis_size("fsdp")
    factor = 1.0 / math.sqrt(total_tokens)
    summed = lax.psum_scatter(
        jnp.dot(local_tokens.T, joined, preferred_element_type=F32) * factor,
        ("fsdp", "seq"),
        scatter_dimension=0,
        tiled=True,
    )
    width_q = w_query.shape[1]
    key_width = w_key.shape[1]
    grad_wq = summed[:, :width_q].astype(BF16)
    grad_wk = summed[:, width_q : width_q + key_width].astype(BF16)
    grad_wv = summed[:, width_q + key_width :].astype(BF16)
    return (attended[None], grad_in.astype(BF16)[None], grad_wq, grad_wk, grad_wv)


def swap(x, axis, j):
    n = lax.axis_size(axis)
    return lax.ppermute(x, axis, [(i, i ^ j) for i in range(n)])


def note_kernel(*refs):
    refs[-1][...] = jnp.zeros_like(refs[-1])


def note(cost, *others):
    return pl.pallas_call(
        note_kernel,
        out_shape=shape(8, 128, dtype=F32),
        in_specs=[pl.BlockSpec(memory_space=pltpu.VMEM)] * len(others),
        out_specs=pl.BlockSpec(memory_space=pltpu.VMEM),
        compiler_params=pltpu.CompilerParams(vmem_limit_bytes=VMEM_LIMIT),
        cost_estimate=pl.CostEstimate(flops=cost << 30, bytes_accessed=0, transcendentals=0),
    )(*others)


def vmem_call(kernel, out_shape, scratch_shapes=(), smem=0, total=0, place=pltpu.VMEM):
    def call(*args):
        in_specs = [
            pl.BlockSpec(memory_space=pltpu.SMEM if i < smem else place)
            for i in range(len(args))
        ]
        return pl.pallas_call(
            kernel,
            out_shape=out_shape,
            in_specs=in_specs,
            out_specs=jax.tree.map(lambda _: pl.BlockSpec(memory_space=pltpu.VMEM), out_shape),
            scratch_shapes=scratch_shapes,
            compiler_params=pltpu.CompilerParams(vmem_limit_bytes=VMEM_LIMIT),
            cost_estimate=pl.CostEstimate(flops=total, bytes_accessed=4 << 20, transcendentals=0),
        )(*args)

    return call


def shape(*dims, dtype=BF16):
    return jax.ShapeDtypeStruct(dims, dtype)


def group_columns(ref, group, width):
    if width % 128 == 0:
        return ref[:, pl.ds(pl.multiple_of(group * width, width), width)]
    per = 128 // width
    wide = ref[:, pl.ds(pl.multiple_of((group // per) * 128, 128), 128)]
    part = wide[:, :width]
    for i in range(1, per):
        part = jnp.where(group % per == i, wide[:, i * width : (i + 1) * width], part)
    return part


def pack_kernel(place_ref, wq_hbm, wk_hbm, wv_hbm, grad_hbm, w_rest, near, *refs):
    outs, held, sem = refs[:3], refs[3:7], refs[7]
    copies = [
        pltpu.make_async_copy(source, target, sem.at[i])
        for i, (source, target) in enumerate(zip((wq_hbm, wk_hbm, wv_hbm, grad_hbm), held))
    ]
    for copy in copies:
        copy.start()
    for copy in copies:
        copy.wait()
    wq_ref, wk_ref, wv_ref, grad_ref = held
    s = place_ref[1]
    wide = wq_ref.shape[1] // 4
    narrow = wk_ref.shape[1] // 4
    joined = wide + 2 * narrow
    depth = wq_ref.shape[0]
    targets = (outs[0], near, outs[1], outs[2])
    spots = (1, 0, 3, 2)
    for j in range(4):
        g = s ^ j
        q = group_columns(wq_ref, g, wide)
        k = group_columns(wk_ref, g, narrow)
        v = group_columns(wv_ref, g, narrow)
        row = jnp.concatenate([q, k, v], axis=1)
        near[:, spots[j] * joined : (spots[j] + 1) * joined] = row
        if j > 0:
            w_rest[:, (j - 1) * joined : j * joined] = row
        if j != 1:
            targets[j][:, :joined] = row
        grad = group_columns(grad_ref, g, wide)
        left = 4 * joined if j == 1 else joined
        for i in range(grad_ref.shape[0] // depth):
            piece = grad[i * depth : (i + 1) * depth]
            targets[j][:, left + i * wide : left + (i + 1) * wide] = piece


def attend_kernel(place_ref, adjacency_ref, *refs):
    f, s = place_ref[0], place_ref[1]
    x_refs, own_ref, other_ref, pay_refs = refs[0:4], refs[4], refs[5], refs[6:10]
    d_refs = refs[11:15]
    w_scr, q_scr, gt_scr = refs[15:18]
    rows = x_refs[0].shape[0]
    length = 4 * rows
    depth, joined = own_ref.shape[2:]
    hs = HEAD_SIZE
    wide = joined - 2 * hs
    per = wide // hs

    for jf in range(8):
        w_ref = own_ref if jf % 2 == 0 else other_ref
        for l in range(4):
            row = pl.multiple_of(((f ^ jf) * 4 + (s ^ l)) * depth, depth)
            w_scr[pl.ds(row, depth), :] = w_ref[jf // 2, l]
    x = jnp.concatenate([r[...] for r in x_refs], axis=0)
    acc = jnp.dot(x, w_scr[...], preferred_element_type=F32)
    low = acc.astype(BF16)
    q_scr[...] = low[:, :wide]
    keys = low[:, wide : wide + hs]
    values = low[:, wide + hs : wide + 2 * hs]
    keys_t = keys.astype(F32).T.astype(BF16)
    values_t = values.astype(F32).T.astype(BF16)
    for j in range(4):
        left = 4 * joined if j == 1 else joined
        for i in range(rows // depth):
            cols = slice(left + i * wide, left + (i + 1) * wide)
            gt_scr[j * rows + i * depth : j * rows + (i + 1) * depth, :] = pay_refs[j][:, cols]

    blocks = length // BLK
    half = rows // BLK

    def absolute(b):
        return (s ^ (b // half)) * half + b % half

    tile = length
    lane_block = lax.broadcasted_iota(jnp.int32, (1, tile), 1) // BLK
    last = (((1,), (1,)), ((), ()))

    def bias_row(b, t):
        row = jnp.zeros((1, tile), F32)
        for c in range(tile // BLK):
            linked = adjacency_ref[absolute(b), absolute(t * (tile // BLK) + c)] > 0
            row = jnp.where(lane_block == c, jnp.where(linked, 0.0, -1e30).astype(F32), row)
        return row

    grad_keys = jnp.zeros((length, hs), F32)
    grad_values = jnp.zeros((length, hs), F32)
    out_t = [[None] * (length // tile) for _ in range(per)]
    dq_t = [[None] * (length // tile) for _ in range(per)]
    for t in range(length // tile):
        bias = jnp.concatenate(
            [jnp.broadcast_to(bias_row(b, t), (BLK, tile)) for b in range(blocks)], axis=0
        )
        for h in range(per):
            q = q_scr[t * tile : (t + 1) * tile, h * hs : (h + 1) * hs]
            g = gt_scr[t * tile : (t + 1) * tile, h * hs : (h + 1) * hs]
            q8 = (q.astype(F32) * 0.125).astype(BF16)
            sc = lax.dot_general(keys, q8, last, preferred_element_type=F32) + bias
            top = jnp.max(sc, axis=0, keepdims=True)
            e = jnp.exp(sc - top)
            p = e * (1.0 / jnp.sum(e, axis=0, keepdims=True))
            p_low = p.astype(BF16)
            dp = lax.dot_general(values, g, last, preferred_element_type=F32)
            inner = jnp.sum(p * dp, axis=0, keepdims=True)
            ds = (p * (dp - inner)).astype(BF16)
            out_t[h][t] = jnp.dot(values_t, p_low, preferred_element_type=F32)
            dq_t[h][t] = jnp.dot(keys_t, ds, preferred_element_type=F32) * 0.125
            grad_keys = grad_keys + jnp.dot(ds, q8, preferred_element_type=F32)
            grad_values = grad_values + jnp.dot(p_low, g, preferred_element_type=F32)
    dkv = jnp.concatenate([grad_keys, grad_values], axis=1).astype(BF16)
    out_t = jnp.concatenate([jnp.concatenate(o, axis=1) for o in out_t], axis=0)
    dq_t = jnp.concatenate([jnp.concatenate(o, axis=1) for o in dq_t], axis=0)
    for j in range(4):
        att = out_t[:, j * rows : (j + 1) * rows].T.astype(BF16)
        dq = dq_t[:, j * rows : (j + 1) * rows].T.astype(BF16)
        block = jnp.concatenate([dq, dkv[j * rows : (j + 1) * rows]], axis=1)
        d_refs[j][:rows, :joined] = block
        d_refs[j ^ 2][rows:, :joined] = block
        d_refs[j][:rows, joined:] = att[:, : wide // 2]
        d_refs[j][rows:, joined:] = att[:, wide // 2 :]


def weight_grad_kernel(parity, place_ref, x0, x1, x2, x3, d0_ref, d1_ref, out_ref):
    f, s = place_ref[0], place_ref[1]
    depth, joined = out_ref.shape[2:]
    span = 4 * depth
    d = jnp.concatenate([d0_ref[:, :joined], d1_ref[:, :joined]], axis=0)
    for i in range(4):
        cols = pl.ds(pl.multiple_of((f ^ (2 * i + parity)) * span, span), span)
        x = jnp.concatenate([r[:, cols] for r in (x0, x2, x1, x3)], axis=0)
        part = lax.dot_general(x, d, (((0,), (0,)), ((), ())), preferred_element_type=F32)
        for k in range(4):
            out_ref[i, s ^ k] = part[k * depth : (k + 1) * depth]


def token_grad_kernel(place_ref, d0, d1, d2, d3, *refs):
    f, s = place_ref[0], place_ref[1]
    group_refs, rest_refs, own_ref, send_ref = refs[:2], refs[2:4], refs[4], refs[5]
    rows = own_ref.shape[0]
    depth, joined = group_refs[0].shape[2:]
    last = (((1,), (1,)), ((), ()))
    d = [r[:, :joined] for r in (d0, d1, d2, d3)]
    sides = []
    for l in range(2):
        first = jnp.concatenate([group_refs[i % 2][i // 2, l] for i in range(8)], axis=0)
        total = lax.dot_general(d[0], first, last, preferred_element_type=F32)
        w = jnp.concatenate([rest_refs[i % 2][i // 2, l] for i in range(8)], axis=0)
        others = jnp.concatenate([d[1], d[2], d[3]], axis=1)
        total = total + lax.dot_general(others, w, last, preferred_element_type=F32)
        sides.append(total.astype(BF16))
    odd = s % 2 == 1
    first = jnp.where(odd, sides[1], sides[0])
    second = jnp.where(odd, sides[0], sides[1])
    for i in range(8):
        part = slice(i * depth, (i + 1) * depth)
        both = jnp.concatenate([first[:, part], second[:, part]], axis=1)
        cols = pl.ds(pl.multiple_of((f ^ i) * 2 * depth, 2 * depth), 2 * depth)
        own_ref[:, cols] = both[:rows]
        send_ref[:, cols] = both[rows:]


def token_join_kernel(place_ref, own_ref, got_ref, out_ref):
    high = place_ref[1] // 2
    part = own_ref.shape[1] // 8
    for i in range(8):
        cols = slice(i * part, (i + 1) * part)
        here = pl.multiple_of((2 * i + high) * part, part)
        there = pl.multiple_of((2 * i + 1 - high) * part, part)
        out_ref[:, pl.ds(here, part)] = own_ref[:, cols]
        out_ref[:, pl.ds(there, part)] = got_ref[:, cols]


def attended_join_kernel(place_ref, d0, d1, d2, d3, out_ref):
    s = place_ref[1]
    rows = out_ref.shape[0]
    part = out_ref.shape[1] // 8
    for j, ref in enumerate((d0, d1, d2, d3)):
        both = jnp.concatenate([ref[:rows, -part:], ref[rows:, -part:]], axis=1)
        out_ref[:, pl.ds(pl.multiple_of((s ^ j) * 2 * part, 2 * part), 2 * part)] = both


def weight_join_kernel(place_ref, b0, b1, b2, b3, q_ref, k_ref, v_ref):
    s = place_ref[1]
    wide = q_ref.shape[1] // 4
    narrow = k_ref.shape[1] // 4
    blocks = [b[...] for b in (b0, b1, b2, b3)]
    for j, b in enumerate(blocks):
        q_ref[:, pl.ds(pl.multiple_of((s ^ j) * wide, wide), wide)] = b[:, :wide]
    odd, high = s % 2 == 1, s // 2 == 1
    tails = [b[:, wide:] for b in blocks]
    one = [jnp.where(odd, tails[i ^ 1], tails[i]) for i in range(4)]
    two = [jnp.where(high, one[i ^ 2], one[i]) for i in range(4)]
    k_ref[...] = jnp.concatenate([b[:, :narrow] for b in two], axis=1)
    v_ref[...] = jnp.concatenate([b[:, narrow:] for b in two], axis=1)


def head_body(tokens, adjacency, w_query, w_key, value_weight, grad_attn):
    x0 = tokens[0]
    rows, width = x0.shape
    depth = w_query.shape[0]
    wide = w_query.shape[1] // 4
    narrow = w_key.shape[1] // 4
    joined = wide + 2 * narrow
    place = jnp.stack([lax.axis_index("fsdp"), lax.axis_index("seq")]).astype(jnp.int32)

    x1 = swap(x0, "seq", 1)
    x2 = swap(x0, "seq", 2)

    few = rows // depth * wide
    w_rest, near, *pay = vmem_call(
        pack_kernel,
        [shape(depth, 3 * joined), shape(depth, 4 * joined + few)]
        + [shape(depth, joined + few)] * 3,
        scratch_shapes=[
            pltpu.VMEM((depth, 4 * wide), BF16),
            pltpu.VMEM((depth, 4 * narrow), BF16),
            pltpu.VMEM((depth, 4 * narrow), BF16),
            pltpu.VMEM((rows, 4 * wide), BF16),
            pltpu.SemaphoreType.DMA((4,)),
        ],
        smem=1,
        place=pltpu.HBM,
    )(place, w_query, w_key, value_weight, grad_attn[0])

    pay = [pay[0], swap(near, "seq", 1), swap(pay[1], "seq", 2), swap(pay[2], "seq", 3)]
    pay, x2 = lax.optimization_barrier((pay, x2))

    w_rows = jnp.stack([p[:, :joined] for p in pay])
    w_own = jnp.stack([w_rows] + [swap(w_rows, "fsdp", j) for j in (2, 4, 6)])
    u_rows = jnp.stack([w_rest, pay[1][:, joined : 4 * joined]])
    w_own, x1 = lax.optimization_barrier((w_own, x1))
    x3 = swap(x2, "seq", 1)
    x3, mark = lax.optimization_barrier((x3, note(8, x3)))
    w_other = swap(w_own, "fsdp", 1)
    u_part = [swap(u_rows, "fsdp", j) for j in (2, 4)]

    d = vmem_call(
        attend_kernel,
        [shape(2 * rows, joined + wide // 2)] * 4,
        scratch_shapes=[
            pltpu.VMEM((width, joined), BF16),
            pltpu.VMEM((4 * rows, wide), BF16),
            pltpu.VMEM((4 * rows, wide), BF16),
        ],
        smem=2,
        total=20 << 30,
    )(place, adjacency, x0, x1, x2, x3, w_own, w_other, *pay, mark)

    def weight_grad(parity, d):
        return vmem_call(
            functools.partial(weight_grad_kernel, parity),
            shape(4, 4, depth, joined, dtype=F32),
            smem=1,
            total=1 << 30,
        )(place, x0, x1, x2, x3, d[0], d[1])

    away = weight_grad(1, d)
    d, away = lax.optimization_barrier((d, away))
    sent = swap(away, "fsdp", 1)
    d_got = {j: swap(d[j], "seq", j) for j in (3, 2, 1)}
    d_got = [d[0], d_got[1], d_got[2], d_got[3]]
    d, u_part = lax.optimization_barrier((d, u_part))
    kept = weight_grad(0, d)
    total = kept + sent
    u_own = jnp.stack([u_rows, *u_part, swap(u_part[0], "fsdp", 4)])
    d_got[2], u_own = lax.optimization_barrier((d_got[2], u_own))
    u_other = swap(u_own, "fsdp", 1)
    got = [swap(total[i], "fsdp", 2 * i) for i in (1, 2, 3)]
    factor = 1.0 / math.sqrt(4 * rows * lax.axis_size("fsdp"))
    summed = (((total[0] + got[0]) + (got[1] + got[2])) * factor).astype(BF16)
    w_final = [summed[0]] + [swap(summed[j], "seq", j) for j in (1, 2, 3)]

    own, send = vmem_call(
        token_grad_kernel,
        [shape(rows, width // 2)] * 2,
        smem=1,
        total=2 << 30,
    )(place, *d_got, w_own, w_other, u_own, u_other)
    half = swap(send, "seq", 2)

    attended = vmem_call(
        attended_join_kernel, shape(rows, 4 * wide)
    )(place, *d_got)
    weights = vmem_call(
        weight_join_kernel,
        [shape(depth, 4 * wide), shape(depth, 4 * narrow), shape(depth, 4 * narrow)],
        smem=1,
    )(place, *w_final)
    grad_wq, grad_wk, grad_wv = weights
    grad_in = vmem_call(token_join_kernel, shape(rows, width), smem=1)(place, own, half)
    return attended[None], grad_in[None], grad_wq, grad_wk, grad_wv


def solution(mesh):
    by_heads = mesh.shape["seq"] == KEY_VALUE_HEADS and mesh.shape["fsdp"] == 8
    return jax.shard_map(
        head_body if by_heads else general_body,
        mesh=mesh,
        in_specs=(
            P("fsdp", "seq", None),
            P(),
            P(("fsdp", "seq"), None),
            P(("fsdp", "seq"), None),
            P(("fsdp", "seq"), None),
            P("fsdp", "seq", None),
        ),
        out_specs=(
            P("fsdp", "seq", None),
            P("fsdp", "seq", None),
            P(("fsdp", "seq"), None),
            P(("fsdp", "seq"), None),
            P(("fsdp", "seq"), None),
        ),
        check_vma=False,
    )
```

```python
import functools
import math

import jax
import jax.numpy as jnp
from jax import lax
from jax.experimental import pallas as pl
from jax.experimental.pallas import tpu as pltpu
from jax.sharding import PartitionSpec as P

KEY_VALUE_HEADS = 4
HEAD_SIZE = 64
BLK = 64
F32 = jnp.float32
BF16 = jnp.bfloat16
VMEM_LIMIT = 48 * 1024 * 1024


def attend_group(query, keys, values, grad_out, allowed):
    scores = jnp.einsum("qhd,kd->hqk", query, keys, preferred_element_type=F32) * 0.125
    scores = jnp.where(allowed[None], scores, jnp.float32(-1e30))
    highest = jnp.max(scores, axis=-1, keepdims=True)
    expo = jnp.exp(scores - highest)
    probs = expo / jnp.sum(expo, axis=-1, keepdims=True)
    probs_low = probs.astype(BF16)
    output = jnp.einsum("hqk,kd->qhd", probs_low, values, preferred_element_type=F32)
    grad_probs = jnp.einsum("qhd,kd->hqk", grad_out, values, preferred_element_type=F32)
    inner = jnp.sum(probs * grad_probs, axis=-1, keepdims=True)
    grad_scores = (probs * (grad_probs - inner) * 0.125).astype(BF16)
    grad_query = jnp.einsum("hqk,kd->qhd", grad_scores, keys, preferred_element_type=F32)
    grad_keys = jnp.einsum("hqk,qhd->kd", grad_scores, query, preferred_element_type=F32)
    grad_values = jnp.einsum("hqk,qhd->kd", probs_low, grad_out, preferred_element_type=F32)
    return (output, grad_query, grad_keys, grad_values)


def general_body(tokens, adjacency, w_query, w_key, value_weight, grad_attn):
    local_tokens = tokens[0]
    local_grad = grad_attn[0]
    rows_here = local_tokens.shape[0]
    full_q, full_k, full_v = (
        lax.all_gather(w_query, ("fsdp", "seq"), axis=0, tiled=True),
        lax.all_gather(w_key, ("fsdp", "seq"), axis=0, tiled=True),
        lax.all_gather(value_weight, ("fsdp", "seq"), axis=0, tiled=True),
    )
    query = jnp.dot(local_tokens, full_q, preferred_element_type=F32).astype(BF16)
    keys = jnp.dot(local_tokens, full_k, preferred_element_type=F32).astype(BF16)
    values = jnp.dot(local_tokens, full_v, preferred_element_type=F32).astype(BF16)
    all_keys, all_values = (
        lax.all_gather(keys, "seq", axis=0, tiled=True),
        lax.all_gather(values, "seq", axis=0, tiled=True),
    )
    blocks_here = rows_here // BLK
    position = lax.axis_index("seq")
    mask_rows = lax.dynamic_slice_in_dim(adjacency, position * blocks_here, blocks_here, 0)
    allowed = jnp.repeat(jnp.repeat(mask_rows, BLK, axis=0), BLK, axis=1) > 0
    group_size = w_query.shape[1] // w_key.shape[1]
    outs_list, dq_list, dk_list, dv_list = ([], [], [], [])
    for head_grouping in range(KEY_VALUE_HEADS):
        low = head_grouping * group_size * HEAD_SIZE
        high = low + group_size * HEAD_SIZE
        group_query = query[:, low:high].reshape(rows_here, group_size, HEAD_SIZE)
        group_grad = local_grad[:, low:high].reshape(rows_here, group_size, HEAD_SIZE)
        group_keys = all_keys[:, head_grouping * HEAD_SIZE : (head_grouping + 1) * HEAD_SIZE]
        group_values = all_values[:, head_grouping * HEAD_SIZE : (head_grouping + 1) * HEAD_SIZE]
        output, grad_query, grad_keys, grad_values = attend_group(
            group_query, group_keys, group_values, group_grad, allowed
        )
        outs_list.append(output.reshape(rows_here, group_size * HEAD_SIZE))
        dq_list.append(grad_query.reshape(rows_here, group_size * HEAD_SIZE))
        dk_list.append(grad_keys)
        dv_list.append(grad_values)
    attended = jnp.concatenate(outs_list, axis=1).astype(BF16)
    grad_query = jnp.concatenate(dq_list, axis=1).astype(BF16)
    key_terms = jnp.concatenate(dk_list, axis=1)
    value_terms = jnp.concatenate(dv_list, axis=1)
    summed_keys, summed_values = (
        lax.psum_scatter(key_terms, "seq", scatter_dimension=0, tiled=True),
        lax.psum_scatter(value_terms, "seq", scatter_dimension=0, tiled=True),
    )
    grad_keys = summed_keys.astype(BF16)
    grad_values = summed_values.astype(BF16)
    grad_in = jnp.dot(grad_query, full_q.T, preferred_element_type=F32)
    grad_in = grad_in + jnp.dot(grad_keys, full_k.T, preferred_element_type=F32)
    grad_in = grad_in + jnp.dot(grad_values, full_v.T, preferred_element_type=F32)
    joined = jnp.concatenate([grad_query, grad_keys, grad_values], axis=1)
    total_tokens = all_keys.shape[0] * lax.axis_size("fsdp")
    factor = 1.0 / math.sqrt(total_tokens)
    summed = lax.psum_scatter(
        jnp.dot(local_tokens.T, joined, preferred_element_type=F32) * factor,
        ("fsdp", "seq"),
        scatter_dimension=0,
        tiled=True,
    )
    width_q = w_query.shape[1]
    key_width = w_key.shape[1]
    grad_wq = summed[:, :width_q].astype(BF16)
    grad_wk = summed[:, width_q : width_q + key_width].astype(BF16)
    grad_wv = summed[:, width_q + key_width :].astype(BF16)
    return (attended[None], grad_in.astype(BF16)[None], grad_wq, grad_wk, grad_wv)


def swap(x, axis, j):
    n = lax.axis_size(axis)
    return lax.ppermute(x, axis, [(i, i ^ j) for i in range(n)])


def note_kernel(*refs):
    refs[-1][...] = jnp.zeros_like(refs[-1])


def note(cost, *others):
    return pl.pallas_call(
        note_kernel,
        out_shape=shape(8, 128, dtype=F32),
        in_specs=[pl.BlockSpec(memory_space=pltpu.VMEM)] * len(others),
        out_specs=pl.BlockSpec(memory_space=pltpu.VMEM),
        compiler_params=pltpu.CompilerParams(vmem_limit_bytes=VMEM_LIMIT),
        cost_estimate=pl.CostEstimate(flops=cost << 30, bytes_accessed=0, transcendentals=0),
    )(*others)


def vmem_call(kernel, out_shape, scratch_shapes=(), smem=0, total=0, place=pltpu.VMEM, limit=VMEM_LIMIT):
    def call(*args):
        in_specs = [
            pl.BlockSpec(memory_space=pltpu.SMEM if i < smem else place)
            for i in range(len(args))
        ]
        return pl.pallas_call(
            kernel,
            out_shape=out_shape,
            in_specs=in_specs,
            out_specs=jax.tree.map(lambda _: pl.BlockSpec(memory_space=pltpu.VMEM), out_shape),
            scratch_shapes=scratch_shapes,
            compiler_params=pltpu.CompilerParams(vmem_limit_bytes=limit),
            cost_estimate=pl.CostEstimate(flops=total, bytes_accessed=4 << 20, transcendentals=0),
        )(*args)

    return call


def shape(*dims, dtype=BF16):
    return jax.ShapeDtypeStruct(dims, dtype)


def group_columns(ref, group, width):
    if width % 128 == 0:
        return ref[:, pl.ds(pl.multiple_of(group * width, width), width)]
    per = 128 // width
    wide = ref[:, pl.ds(pl.multiple_of((group // per) * 128, 128), 128)]
    part = wide[:, :width]
    for i in range(1, per):
        part = jnp.where(group % per == i, wide[:, i * width : (i + 1) * width], part)
    return part


def pack_kernel(place_ref, wq_hbm, wk_hbm, wv_hbm, grad_hbm, w_rest, near, *refs):
    outs, held, sem = refs[:3], refs[3:7], refs[7]
    copies = [
        pltpu.make_async_copy(source, target, sem.at[i])
        for i, (source, target) in enumerate(zip((wq_hbm, wk_hbm, wv_hbm, grad_hbm), held))
    ]
    for copy in copies:
        copy.start()
    for copy in copies:
        copy.wait()
    wq_ref, wk_ref, wv_ref, grad_ref = held
    s = place_ref[1]
    wide = wq_ref.shape[1] // 4
    narrow = wk_ref.shape[1] // 4
    joined = wide + 2 * narrow
    depth = wq_ref.shape[0]
    targets = (outs[0], near, outs[1], outs[2])
    spots = (1, 0, 3, 2)
    for j in range(4):
        g = s ^ j
        q = group_columns(wq_ref, g, wide)
        k = group_columns(wk_ref, g, narrow)
        v = group_columns(wv_ref, g, narrow)
        row = jnp.concatenate([q, k, v], axis=1)
        near[:, spots[j] * joined : (spots[j] + 1) * joined] = row
        if j > 0:
            w_rest[:, (j - 1) * joined : j * joined] = row
        if j != 1:
            targets[j][:, :joined] = row
        grad = group_columns(grad_ref, g, wide)
        left = 4 * joined if j == 1 else joined
        for i in range(grad_ref.shape[0] // depth):
            piece = grad[i * depth : (i + 1) * depth]
            targets[j][:, left + i * wide : left + (i + 1) * wide] = piece


def attend_kernel(place_ref, adjacency_ref, *refs):
    f, s = place_ref[0], place_ref[1]
    x_refs, own_ref, other_ref, pay_refs = refs[0:4], refs[4], refs[5], refs[6:10]
    d_refs = refs[11:14]
    w_scr, q_scr, gt_scr = refs[-3:]
    rows = x_refs[0].shape[0]
    length = 4 * rows
    depth, joined = own_ref.shape[2:]
    hs = HEAD_SIZE
    wide = joined - 2 * hs
    per = wide // hs

    for jf in range(8):
        w_ref = own_ref if jf % 2 == 0 else other_ref
        for l in range(4):
            row = pl.multiple_of(((f ^ jf) * 4 + (s ^ l)) * depth, depth)
            w_scr[pl.ds(row, depth), :] = w_ref[jf // 2, l]
    x = jnp.concatenate([r[...] for r in x_refs], axis=0)
    acc = jnp.dot(x, w_scr[...], preferred_element_type=F32)
    low = acc.astype(BF16)
    q_scr[...] = low[:, :wide]
    keys = low[:, wide : wide + hs]
    values = low[:, wide + hs : wide + 2 * hs]
    keys_t = keys.astype(F32).T.astype(BF16)
    values_t = values.astype(F32).T.astype(BF16)
    for j in range(4):
        left = 4 * joined if j == 1 else joined
        for i in range(rows // depth):
            cols = slice(left + i * wide, left + (i + 1) * wide)
            gt_scr[j * rows + i * depth : j * rows + (i + 1) * depth, :] = pay_refs[j][:, cols]

    blocks = length // BLK
    half = rows // BLK

    def absolute(b):
        return (s ^ (b // half)) * half + b % half

    tile = length
    lane_block = lax.broadcasted_iota(jnp.int32, (1, tile), 1) // BLK
    last = (((1,), (1,)), ((), ()))

    def bias_row(b, t):
        row = jnp.zeros((1, tile), F32)
        for c in range(tile // BLK):
            linked = adjacency_ref[absolute(b), absolute(t * (tile // BLK) + c)] > 0
            row = jnp.where(lane_block == c, jnp.where(linked, 0.0, -1e30).astype(F32), row)
        return row

    grad_keys = jnp.zeros((length, hs), F32)
    grad_values = jnp.zeros((length, hs), F32)
    out_t = [[None] * (length // tile) for _ in range(per)]
    dq_t = [[None] * (length // tile) for _ in range(per)]
    for t in range(length // tile):
        bias = jnp.concatenate(
            [jnp.broadcast_to(bias_row(b, t), (BLK, tile)) for b in range(blocks)], axis=0
        )
        for h in range(per):
            q = q_scr[t * tile : (t + 1) * tile, h * hs : (h + 1) * hs]
            g = gt_scr[t * tile : (t + 1) * tile, h * hs : (h + 1) * hs]
            q8 = (q.astype(F32) * 0.125).astype(BF16)
            sc = lax.dot_general(keys, q8, last, preferred_element_type=F32) + bias
            top = jnp.max(sc, axis=0, keepdims=True)
            e = jnp.exp(sc - top)
            p = e * (1.0 / jnp.sum(e, axis=0, keepdims=True))
            p_low = p.astype(BF16)
            dp = lax.dot_general(values, g, last, preferred_element_type=F32)
            inner = jnp.sum(p * dp, axis=0, keepdims=True)
            ds = (p * (dp - inner)).astype(BF16)
            out_t[h][t] = jnp.dot(values_t, p_low, preferred_element_type=F32)
            dq_t[h][t] = jnp.dot(keys_t, ds, preferred_element_type=F32) * 0.125
            grad_keys = grad_keys + jnp.dot(ds, q8, preferred_element_type=F32)
            grad_values = grad_values + jnp.dot(p_low, g, preferred_element_type=F32)
    dkv = jnp.concatenate([grad_keys, grad_values], axis=1).astype(BF16)
    out_t = jnp.concatenate([jnp.concatenate(o, axis=1) for o in out_t], axis=0)
    dq_t = jnp.concatenate([jnp.concatenate(o, axis=1) for o in dq_t], axis=0)
    for j in range(4):
        att = out_t[:, j * rows : (j + 1) * rows].T.astype(BF16)
        dq = dq_t[:, j * rows : (j + 1) * rows].T.astype(BF16)
        block = jnp.concatenate([dq, dkv[j * rows : (j + 1) * rows]], axis=1)
        if j < 3:
            d_refs[j][:rows, :joined] = block
        if j != 1:
            d_refs[j ^ 2][rows:, :joined] = block
        spot = d_refs[j] if j < 3 else d_refs[1]
        left = joined if j < 3 else joined + wide // 2
        spot[:rows, left : left + wide // 2] = att[:, : wide // 2]
        spot[rows:, left : left + wide // 2] = att[:, wide // 2 :]


def weight_grad_kernel(parity, place_ref, x0, x1, x2, x3, d0_ref, d1_ref, out_ref):
    f, s = place_ref[0], place_ref[1]
    depth, joined = out_ref.shape[2:]
    span = 4 * depth
    d = jnp.concatenate([d0_ref[:, :joined], d1_ref[:, :joined]], axis=0)
    for i in range(4):
        cols = pl.ds(pl.multiple_of((f ^ (2 * i + parity)) * span, span), span)
        x = jnp.concatenate([r[:, cols] for r in (x0, x2, x1, x3)], axis=0)
        part = lax.dot_general(x, d, (((0,), (0,)), ((), ())), preferred_element_type=F32)
        for k in range(4):
            out_ref[i, s ^ k] = part[k * depth : (k + 1) * depth]


def token_grad_kernel(place_ref, d0, d1, d2, d3, *refs):
    f, s = place_ref[0], place_ref[1]
    group_refs, rest_refs, own_ref, send_ref = refs[:2], refs[2:4], refs[4], refs[5]
    rows = own_ref.shape[0]
    depth, joined = group_refs[0].shape[2:]
    last = (((1,), (1,)), ((), ()))
    d = [r[:, :joined] for r in (d0, d1, d2, d3)]
    d[3] = jnp.concatenate([d[3][rows:], d[3][:rows]], axis=0)
    sides = []
    for l in range(2):
        first = jnp.concatenate([group_refs[i % 2][i // 2, l] for i in range(8)], axis=0)
        total = lax.dot_general(d[0], first, last, preferred_element_type=F32)
        w = jnp.concatenate([rest_refs[i % 2][i // 2, l] for i in range(8)], axis=0)
        others = jnp.concatenate([d[1], d[2], d[3]], axis=1)
        total = total + lax.dot_general(others, w, last, preferred_element_type=F32)
        sides.append(total.astype(BF16))
    odd = s % 2 == 1
    first = jnp.where(odd, sides[1], sides[0])
    second = jnp.where(odd, sides[0], sides[1])
    for i in range(8):
        part = slice(i * depth, (i + 1) * depth)
        both = jnp.concatenate([first[:, part], second[:, part]], axis=1)
        cols = pl.ds(pl.multiple_of((f ^ i) * 2 * depth, 2 * depth), 2 * depth)
        own_ref[:, cols] = both[:rows]
        send_ref[:, cols] = both[rows:]


def token_join_kernel(place_ref, own_ref, got_ref, out_ref):
    high = place_ref[1] // 2
    part = own_ref.shape[1] // 8
    for i in range(8):
        cols = slice(i * part, (i + 1) * part)
        here = pl.multiple_of((2 * i + high) * part, part)
        there = pl.multiple_of((2 * i + 1 - high) * part, part)
        out_ref[:, pl.ds(here, part)] = own_ref[:, cols]
        out_ref[:, pl.ds(there, part)] = got_ref[:, cols]


def attended_join_kernel(place_ref, d0, d1, d2, d3, out_ref):
    s = place_ref[1]
    rows = out_ref.shape[0]
    part = out_ref.shape[1] // 8
    for j, ref in enumerate((d0, d1, d2, d3)):
        here = slice(3 * part, 4 * part)
        both = jnp.concatenate([ref[:rows, here], ref[rows:, here]], axis=1)
        out_ref[:, pl.ds(pl.multiple_of((s ^ j) * 2 * part, 2 * part), 2 * part)] = both


def weight_join_kernel(place_ref, b0, b1, b2, b3, q_ref, k_ref, v_ref):
    s = place_ref[1]
    wide = q_ref.shape[1] // 4
    narrow = k_ref.shape[1] // 4
    blocks = [b[...] for b in (b0, b1, b2, b3)]
    for j, b in enumerate(blocks):
        q_ref[:, pl.ds(pl.multiple_of((s ^ j) * wide, wide), wide)] = b[:, :wide]
    odd, high = s % 2 == 1, s // 2 == 1
    tails = [b[:, wide:] for b in blocks]
    one = [jnp.where(odd, tails[i ^ 1], tails[i]) for i in range(4)]
    two = [jnp.where(high, one[i ^ 2], one[i]) for i in range(4)]
    k_ref[...] = jnp.concatenate([b[:, :narrow] for b in two], axis=1)
    v_ref[...] = jnp.concatenate([b[:, narrow:] for b in two], axis=1)


def join_kernel(place_ref, b0, b1, b2, b3, own, got, q_ref, k_ref, v_ref, out_ref):
    token_join_kernel(place_ref, own, got, out_ref)
    weight_join_kernel(place_ref, b0, b1, b2, b3, q_ref, k_ref, v_ref)


def head_body(tokens, adjacency, w_query, w_key, value_weight, grad_attn):
    x0 = tokens[0]
    rows, width = x0.shape
    depth = w_query.shape[0]
    wide = w_query.shape[1] // 4
    narrow = w_key.shape[1] // 4
    joined = wide + 2 * narrow
    place = jnp.stack([lax.axis_index("fsdp"), lax.axis_index("seq")]).astype(jnp.int32)

    x1 = swap(x0, "seq", 1)
    x2 = swap(x0, "seq", 2)

    few = rows // depth * wide
    w_rest, near, *pay = vmem_call(
        pack_kernel,
        [shape(depth, 3 * joined), shape(depth, 4 * joined + few)]
        + [shape(depth, joined + few)] * 3,
        scratch_shapes=[
            pltpu.VMEM((depth, 4 * wide), BF16),
            pltpu.VMEM((depth, 4 * narrow), BF16),
            pltpu.VMEM((depth, 4 * narrow), BF16),
            pltpu.VMEM((rows, 4 * wide), BF16),
            pltpu.SemaphoreType.DMA((4,)),
        ],
        smem=1,
        place=pltpu.HBM,
    )(place, w_query, w_key, value_weight, grad_attn[0])

    pay = [pay[0], swap(near, "seq", 1), swap(pay[1], "seq", 2), swap(pay[2], "seq", 3)]
    pay, x2 = lax.optimization_barrier((pay, x2))

    w_rows = jnp.stack([p[:, :joined] for p in pay])
    w_own = jnp.stack([w_rows] + [swap(w_rows, "fsdp", j) for j in (2, 4, 6)])
    u_rows = jnp.stack([w_rest, pay[1][:, joined : 4 * joined]])
    w_own, x1 = lax.optimization_barrier((w_own, x1))
    x3 = swap(x2, "seq", 1)
    x3, mark = lax.optimization_barrier((x3, note(8, x3)))
    w_other = swap(w_own, "fsdp", 1)
    u_part = [swap(u_rows, "fsdp", j) for j in (2, 4)]

    d = vmem_call(
        attend_kernel,
        [shape(2 * rows, joined + extra * (wide // 2)) for extra in (1, 2, 1)],
        scratch_shapes=[
            pltpu.VMEM((width, joined), BF16),
            pltpu.VMEM((4 * rows, wide), BF16),
            pltpu.VMEM((4 * rows, wide), BF16),
        ],
        smem=2,
        total=8 << 30,
    )(place, adjacency, x0, x1, x2, x3, w_own, w_other, *pay, mark)

    def weight_grad(parity, d):
        return vmem_call(
            functools.partial(weight_grad_kernel, parity),
            shape(4, 4, depth, joined, dtype=F32),
            smem=1,
            total=8 << 30,
        )(place, x0, x1, x2, x3, d[0], d[1])

    away = weight_grad(1, d)
    d, away = lax.optimization_barrier((d, away))
    sent = swap(away, "fsdp", 1)
    d_two = swap(d[2], "seq", 2)
    d_got = [d[0], swap(d[1], "seq", 1), d_two]
    onward = [d_got[1][:, :joined], d_got[1][:, joined + wide // 2 :]]
    onward = jnp.concatenate(onward, axis=1)
    d_got.append(swap(onward, "seq", 2))
    d, u_part = lax.optimization_barrier((d, u_part))
    kept = weight_grad(0, d)
    total = kept + sent
    u_own = jnp.stack([u_rows, *u_part, swap(u_part[0], "fsdp", 4)])
    u_other = swap(u_own, "fsdp", 1)
    got = [swap(total[i], "fsdp", 2 * i) for i in (1, 2, 3)]
    factor = 1.0 / math.sqrt(4 * rows * lax.axis_size("fsdp"))
    summed = (((total[0] + got[0]) + (got[1] + got[2])) * factor).astype(BF16)
    w_final = [summed[0]] + [swap(summed[j], "seq", j) for j in (1, 2, 3)]

    own, send = vmem_call(
        token_grad_kernel,
        [shape(rows, width // 2)] * 2,
        smem=1,
        total=2 << 30,
    )(place, *d_got, w_own, w_other, u_own, u_other)
    half = swap(send, "seq", 2)

    attended = vmem_call(
        attended_join_kernel, shape(rows, 4 * wide), smem=1
    )(place, *d_got)
    grad_wq, grad_wk, grad_wv, grad_in = vmem_call(
        join_kernel,
        [shape(depth, 4 * wide), shape(depth, 4 * narrow), shape(depth, 4 * narrow)]
        + [shape(rows, width)],
        smem=1,
    )(place, *w_final, own, half)
    return attended[None], grad_in[None], grad_wq, grad_wk, grad_wv


def solution(mesh):
    by_heads = mesh.shape["seq"] == KEY_VALUE_HEADS and mesh.shape["fsdp"] == 8
    return jax.shard_map(
        head_body if by_heads else general_body,
        mesh=mesh,
        in_specs=(
            P("fsdp", "seq", None),
            P(),
            P(("fsdp", "seq"), None),
            P(("fsdp", "seq"), None),
            P(("fsdp", "seq"), None),
            P("fsdp", "seq", None),
        ),
        out_specs=(
            P("fsdp", "seq", None),
            P("fsdp", "seq", None),
            P(("fsdp", "seq"), None),
            P(("fsdp", "seq"), None),
            P(("fsdp", "seq"), None),
        ),
        check_vma=False,
    )
```

```python
import functools
import math

import jax
import jax.numpy as jnp
from jax import lax
from jax.experimental import pallas as pl
from jax.experimental.pallas import tpu as pltpu
from jax.sharding import PartitionSpec as P

KEY_VALUE_HEADS = 4
HEAD_SIZE = 64
BLK = 64
F32 = jnp.float32
BF16 = jnp.bfloat16
VMEM_LIMIT = 48 * 1024 * 1024


def attend_group(query, keys, values, grad_out, allowed):
    scores = jnp.einsum("qhd,kd->hqk", query, keys, preferred_element_type=F32) * 0.125
    scores = jnp.where(allowed[None], scores, jnp.float32(-1e30))
    highest = jnp.max(scores, axis=-1, keepdims=True)
    expo = jnp.exp(scores - highest)
    probs = expo / jnp.sum(expo, axis=-1, keepdims=True)
    probs_low = probs.astype(BF16)
    output = jnp.einsum("hqk,kd->qhd", probs_low, values, preferred_element_type=F32)
    grad_probs = jnp.einsum("qhd,kd->hqk", grad_out, values, preferred_element_type=F32)
    inner = jnp.sum(probs * grad_probs, axis=-1, keepdims=True)
    grad_scores = (probs * (grad_probs - inner) * 0.125).astype(BF16)
    grad_query = jnp.einsum("hqk,kd->qhd", grad_scores, keys, preferred_element_type=F32)
    grad_keys = jnp.einsum("hqk,qhd->kd", grad_scores, query, preferred_element_type=F32)
    grad_values = jnp.einsum("hqk,qhd->kd", probs_low, grad_out, preferred_element_type=F32)
    return (output, grad_query, grad_keys, grad_values)


def general_body(tokens, adjacency, w_query, w_key, value_weight, grad_attn):
    local_tokens = tokens[0]
    local_grad = grad_attn[0]
    rows_here = local_tokens.shape[0]
    full_q, full_k, full_v = (
        lax.all_gather(w_query, ("fsdp", "seq"), axis=0, tiled=True),
        lax.all_gather(w_key, ("fsdp", "seq"), axis=0, tiled=True),
        lax.all_gather(value_weight, ("fsdp", "seq"), axis=0, tiled=True),
    )
    query = jnp.dot(local_tokens, full_q, preferred_element_type=F32).astype(BF16)
    keys = jnp.dot(local_tokens, full_k, preferred_element_type=F32).astype(BF16)
    values = jnp.dot(local_tokens, full_v, preferred_element_type=F32).astype(BF16)
    all_keys, all_values = (
        lax.all_gather(keys, "seq", axis=0, tiled=True),
        lax.all_gather(values, "seq", axis=0, tiled=True),
    )
    blocks_here = rows_here // BLK
    position = lax.axis_index("seq")
    mask_rows = lax.dynamic_slice_in_dim(adjacency, position * blocks_here, blocks_here, 0)
    allowed = jnp.repeat(jnp.repeat(mask_rows, BLK, axis=0), BLK, axis=1) > 0
    group_size = w_query.shape[1] // w_key.shape[1]
    outs_list, dq_list, dk_list, dv_list = ([], [], [], [])
    for head_grouping in range(KEY_VALUE_HEADS):
        low = head_grouping * group_size * HEAD_SIZE
        high = low + group_size * HEAD_SIZE
        group_query = query[:, low:high].reshape(rows_here, group_size, HEAD_SIZE)
        group_grad = local_grad[:, low:high].reshape(rows_here, group_size, HEAD_SIZE)
        group_keys = all_keys[:, head_grouping * HEAD_SIZE : (head_grouping + 1) * HEAD_SIZE]
        group_values = all_values[:, head_grouping * HEAD_SIZE : (head_grouping + 1) * HEAD_SIZE]
        output, grad_query, grad_keys, grad_values = attend_group(
            group_query, group_keys, group_values, group_grad, allowed
        )
        outs_list.append(output.reshape(rows_here, group_size * HEAD_SIZE))
        dq_list.append(grad_query.reshape(rows_here, group_size * HEAD_SIZE))
        dk_list.append(grad_keys)
        dv_list.append(grad_values)
    attended = jnp.concatenate(outs_list, axis=1).astype(BF16)
    grad_query = jnp.concatenate(dq_list, axis=1).astype(BF16)
    key_terms = jnp.concatenate(dk_list, axis=1)
    value_terms = jnp.concatenate(dv_list, axis=1)
    summed_keys, summed_values = (
        lax.psum_scatter(key_terms, "seq", scatter_dimension=0, tiled=True),
        lax.psum_scatter(value_terms, "seq", scatter_dimension=0, tiled=True),
    )
    grad_keys = summed_keys.astype(BF16)
    grad_values = summed_values.astype(BF16)
    grad_in = jnp.dot(grad_query, full_q.T, preferred_element_type=F32)
    grad_in = grad_in + jnp.dot(grad_keys, full_k.T, preferred_element_type=F32)
    grad_in = grad_in + jnp.dot(grad_values, full_v.T, preferred_element_type=F32)
    joined = jnp.concatenate([grad_query, grad_keys, grad_values], axis=1)
    total_tokens = all_keys.shape[0] * lax.axis_size("fsdp")
    factor = 1.0 / math.sqrt(total_tokens)
    summed = lax.psum_scatter(
        jnp.dot(local_tokens.T, joined, preferred_element_type=F32) * factor,
        ("fsdp", "seq"),
        scatter_dimension=0,
        tiled=True,
    )
    width_q = w_query.shape[1]
    key_width = w_key.shape[1]
    grad_wq = summed[:, :width_q].astype(BF16)
    grad_wk = summed[:, width_q : width_q + key_width].astype(BF16)
    grad_wv = summed[:, width_q + key_width :].astype(BF16)
    return (attended[None], grad_in.astype(BF16)[None], grad_wq, grad_wk, grad_wv)


def swap(x, axis, j):
    n = lax.axis_size(axis)
    return lax.ppermute(x, axis, [(i, i ^ j) for i in range(n)])


def note_kernel(*refs):
    refs[-1][...] = jnp.zeros_like(refs[-1])


def note(cost, *others):
    return pl.pallas_call(
        note_kernel,
        out_shape=shape(8, 128, dtype=F32),
        in_specs=[pl.BlockSpec(memory_space=pltpu.VMEM)] * len(others),
        out_specs=pl.BlockSpec(memory_space=pltpu.VMEM),
        compiler_params=pltpu.CompilerParams(vmem_limit_bytes=VMEM_LIMIT),
        cost_estimate=pl.CostEstimate(flops=cost << 30, bytes_accessed=0, transcendentals=0),
    )(*others)


def vmem_call(kernel, out_shape, scratch_shapes=(), smem=0, total=0, place=pltpu.VMEM, limit=VMEM_LIMIT):
    def call(*args):
        in_specs = [
            pl.BlockSpec(memory_space=pltpu.SMEM if i < smem else place)
            for i in range(len(args))
        ]
        return pl.pallas_call(
            kernel,
            out_shape=out_shape,
            in_specs=in_specs,
            out_specs=jax.tree.map(lambda _: pl.BlockSpec(memory_space=pltpu.VMEM), out_shape),
            scratch_shapes=scratch_shapes,
            compiler_params=pltpu.CompilerParams(vmem_limit_bytes=limit),
            cost_estimate=pl.CostEstimate(flops=total, bytes_accessed=4 << 20, transcendentals=0),
        )(*args)

    return call


def shape(*dims, dtype=BF16):
    return jax.ShapeDtypeStruct(dims, dtype)


def group_columns(ref, group, width):
    if width % 128 == 0:
        return ref[:, pl.ds(pl.multiple_of(group * width, width), width)]
    per = 128 // width
    wide = ref[:, pl.ds(pl.multiple_of((group // per) * 128, 128), 128)]
    part = wide[:, :width]
    for i in range(1, per):
        part = jnp.where(group % per == i, wide[:, i * width : (i + 1) * width], part)
    return part


def pack_kernel(place_ref, wq_hbm, wk_hbm, wv_hbm, grad_hbm, w_rest, near, *refs):
    outs, held, sem = refs[:3], refs[3:7], refs[7]
    copies = [
        pltpu.make_async_copy(source, target, sem.at[i])
        for i, (source, target) in enumerate(zip((wq_hbm, wk_hbm, wv_hbm, grad_hbm), held))
    ]
    for copy in copies:
        copy.start()
    for copy in copies:
        copy.wait()
    wq_ref, wk_ref, wv_ref, grad_ref = held
    s = place_ref[1]
    wide = wq_ref.shape[1] // 4
    narrow = wk_ref.shape[1] // 4
    joined = wide + 2 * narrow
    depth = wq_ref.shape[0]
    targets = (outs[0], near, outs[1], outs[2])
    spots = (1, 0, 3, 2)
    for j in range(4):
        g = s ^ j
        q = group_columns(wq_ref, g, wide)
        k = group_columns(wk_ref, g, narrow)
        v = group_columns(wv_ref, g, narrow)
        row = jnp.concatenate([q, k, v], axis=1)
        near[:, spots[j] * joined : (spots[j] + 1) * joined] = row
        if j > 0:
            w_rest[:, (j - 1) * joined : j * joined] = row
        if j != 1:
            targets[j][:, :joined] = row
        grad = group_columns(grad_ref, g, wide)
        left = 4 * joined if j == 1 else joined
        for i in range(grad_ref.shape[0] // depth):
            piece = grad[i * depth : (i + 1) * depth]
            targets[j][:, left + i * wide : left + (i + 1) * wide] = piece


def attend_kernel(place_ref, adjacency_ref, *refs):
    f, s = place_ref[0], place_ref[1]
    x_refs, own_ref, other_ref, pay_refs = refs[0:4], refs[4], refs[5], refs[6:10]
    d_refs = refs[11:14]
    w_scr, q_scr, gt_scr = refs[-3:]
    rows = x_refs[0].shape[0]
    length = 4 * rows
    depth, joined = own_ref.shape[2:]
    hs = HEAD_SIZE
    wide = joined - 2 * hs
    per = wide // hs

    for jf in range(8):
        w_ref = own_ref if jf % 2 == 0 else other_ref
        for l in range(4):
            row = pl.multiple_of(((f ^ jf) * 4 + (s ^ l)) * depth, depth)
            w_scr[pl.ds(row, depth), :] = w_ref[jf // 2, l]
    x = jnp.concatenate([r[...] for r in x_refs], axis=0)
    acc = jnp.dot(x, w_scr[...], preferred_element_type=F32)
    low = acc.astype(BF16)
    q_scr[...] = low[:, :wide]
    keys = low[:, wide : wide + hs]
    values = low[:, wide + hs : wide + 2 * hs]
    keys_t = keys.astype(F32).T.astype(BF16)
    values_t = values.astype(F32).T.astype(BF16)
    for j in range(4):
        left = 4 * joined if j == 1 else joined
        for i in range(rows // depth):
            cols = slice(left + i * wide, left + (i + 1) * wide)
            gt_scr[j * rows + i * depth : j * rows + (i + 1) * depth, :] = pay_refs[j][:, cols]

    blocks = length // BLK
    half = rows // BLK

    def absolute(b):
        return (s ^ (b // half)) * half + b % half

    tile = length
    lane_block = lax.broadcasted_iota(jnp.int32, (1, tile), 1) // BLK
    last = (((1,), (1,)), ((), ()))

    def bias_row(b, t):
        row = jnp.zeros((1, tile), F32)
        for c in range(tile // BLK):
            linked = adjacency_ref[absolute(b), absolute(t * (tile // BLK) + c)] > 0
            row = jnp.where(lane_block == c, jnp.where(linked, 0.0, -1e30).astype(F32), row)
        return row

    grad_keys = jnp.zeros((length, hs), F32)
    grad_values = jnp.zeros((length, hs), F32)
    out_t = [[None] * (length // tile) for _ in range(per)]
    dq_t = [[None] * (length // tile) for _ in range(per)]
    for t in range(length // tile):
        bias = jnp.concatenate(
            [jnp.broadcast_to(bias_row(b, t), (BLK, tile)) for b in range(blocks)], axis=0
        )
        for h in range(per):
            q = q_scr[t * tile : (t + 1) * tile, h * hs : (h + 1) * hs]
            g = gt_scr[t * tile : (t + 1) * tile, h * hs : (h + 1) * hs]
            q8 = (q.astype(F32) * 0.125).astype(BF16)
            sc = lax.dot_general(keys, q8, last, preferred_element_type=F32) + bias
            top = jnp.max(sc, axis=0, keepdims=True)
            e = jnp.exp(sc - top)
            p = e * (1.0 / jnp.sum(e, axis=0, keepdims=True))
            p_low = p.astype(BF16)
            dp = lax.dot_general(values, g, last, preferred_element_type=F32)
            inner = jnp.sum(p * dp, axis=0, keepdims=True)
            ds = (p * (dp - inner)).astype(BF16)
            out_t[h][t] = jnp.dot(values_t, p_low, preferred_element_type=F32)
            dq_t[h][t] = jnp.dot(keys_t, ds, preferred_element_type=F32) * 0.125
            grad_keys = grad_keys + jnp.dot(ds, q8, preferred_element_type=F32)
            grad_values = grad_values + jnp.dot(p_low, g, preferred_element_type=F32)
    dkv = jnp.concatenate([grad_keys, grad_values], axis=1).astype(BF16)
    out_t = jnp.concatenate([jnp.concatenate(o, axis=1) for o in out_t], axis=0)
    dq_t = jnp.concatenate([jnp.concatenate(o, axis=1) for o in dq_t], axis=0)
    for j in range(4):
        att = out_t[:, j * rows : (j + 1) * rows].T.astype(BF16)
        dq = dq_t[:, j * rows : (j + 1) * rows].T.astype(BF16)
        block = jnp.concatenate([dq, dkv[j * rows : (j + 1) * rows]], axis=1)
        if j < 3:
            d_refs[j][:rows, :joined] = block
        if j != 1:
            d_refs[j ^ 2][rows:, :joined] = block
        spot = d_refs[j] if j < 3 else d_refs[1]
        left = joined if j < 3 else joined + wide // 2
        spot[:rows, left : left + wide // 2] = att[:, : wide // 2]
        spot[rows:, left : left + wide // 2] = att[:, wide // 2 :]


def weight_grad_kernel(parity, place_ref, x0, x1, x2, x3, d0_ref, d1_ref, out_ref):
    f, s = place_ref[0], place_ref[1]
    depth, joined = out_ref.shape[2:]
    span = 4 * depth
    d = jnp.concatenate([d0_ref[:, :joined], d1_ref[:, :joined]], axis=0)
    for i in range(4):
        cols = pl.ds(pl.multiple_of((f ^ (2 * i + parity)) * span, span), span)
        x = jnp.concatenate([r[:, cols] for r in (x0, x2, x1, x3)], axis=0)
        part = lax.dot_general(x, d, (((0,), (0,)), ((), ())), preferred_element_type=F32)
        for k in range(4):
            out_ref[i, s ^ k] = part[k * depth : (k + 1) * depth]


def token_grad_kernel(place_ref, d0, d1, d2, d3, *refs):
    f, s = place_ref[0], place_ref[1]
    group_refs, rest_refs, own_ref, send_ref = refs[:2], refs[2:4], refs[5], refs[6]
    rows = own_ref.shape[0]
    depth, joined = group_refs[0].shape[2:]
    last = (((1,), (1,)), ((), ()))
    d = [r[:, :joined] for r in (d0, d1, d2, d3)]
    d[3] = jnp.concatenate([d[3][rows:], d[3][:rows]], axis=0)
    sides = []
    for l in range(2):
        first = jnp.concatenate([group_refs[i % 2][i // 2, l] for i in range(8)], axis=0)
        total = lax.dot_general(d[0], first, last, preferred_element_type=F32)
        w = jnp.concatenate([rest_refs[i % 2][i // 2, l] for i in range(8)], axis=0)
        others = jnp.concatenate([d[1], d[2], d[3]], axis=1)
        total = total + lax.dot_general(others, w, last, preferred_element_type=F32)
        sides.append(total.astype(BF16))
    odd = s % 2 == 1
    first = jnp.where(odd, sides[1], sides[0])
    second = jnp.where(odd, sides[0], sides[1])
    for i in range(8):
        part = slice(i * depth, (i + 1) * depth)
        both = jnp.concatenate([first[:, part], second[:, part]], axis=1)
        cols = pl.ds(pl.multiple_of((f ^ i) * 2 * depth, 2 * depth), 2 * depth)
        own_ref[:, cols] = both[:rows]
        send_ref[:, cols] = both[rows:]


def token_join_kernel(place_ref, own_ref, got_ref, out_ref):
    high = place_ref[1] // 2
    part = own_ref.shape[1] // 8
    for i in range(8):
        cols = slice(i * part, (i + 1) * part)
        here = pl.multiple_of((2 * i + high) * part, part)
        there = pl.multiple_of((2 * i + 1 - high) * part, part)
        out_ref[:, pl.ds(here, part)] = own_ref[:, cols]
        out_ref[:, pl.ds(there, part)] = got_ref[:, cols]


def attended_join_kernel(place_ref, d0, d1, d2, d3, out_ref):
    s = place_ref[1]
    rows = out_ref.shape[0]
    part = out_ref.shape[1] // 8
    for j, ref in enumerate((d0, d1, d2, d3)):
        here = slice(3 * part, 4 * part)
        both = jnp.concatenate([ref[:rows, here], ref[rows:, here]], axis=1)
        out_ref[:, pl.ds(pl.multiple_of((s ^ j) * 2 * part, 2 * part), 2 * part)] = both


def weight_join_kernel(place_ref, b0, b1, b2, b3, _, q_ref, k_ref, v_ref):
    s = place_ref[1]
    wide = q_ref.shape[1] // 4
    narrow = k_ref.shape[1] // 4
    blocks = [b[...] for b in (b0, b1, b2, b3)]
    for j, b in enumerate(blocks):
        q_ref[:, pl.ds(pl.multiple_of((s ^ j) * wide, wide), wide)] = b[:, :wide]
    odd, high = s % 2 == 1, s // 2 == 1
    tails = [b[:, wide:] for b in blocks]
    one = [jnp.where(odd, tails[i ^ 1], tails[i]) for i in range(4)]
    two = [jnp.where(high, one[i ^ 2], one[i]) for i in range(4)]
    k_ref[...] = jnp.concatenate([b[:, :narrow] for b in two], axis=1)
    v_ref[...] = jnp.concatenate([b[:, narrow:] for b in two], axis=1)


def join_kernel(place_ref, b0, b1, b2, b3, mark, own, got, q_ref, k_ref, v_ref, out_ref):
    token_join_kernel(place_ref, own, got, out_ref)
    weight_join_kernel(place_ref, b0, b1, b2, b3, mark, q_ref, k_ref, v_ref)


def head_body(tokens, adjacency, w_query, w_key, value_weight, grad_attn):
    x0 = tokens[0]
    rows, width = x0.shape
    depth = w_query.shape[0]
    wide = w_query.shape[1] // 4
    narrow = w_key.shape[1] // 4
    joined = wide + 2 * narrow
    place = jnp.stack([lax.axis_index("fsdp"), lax.axis_index("seq")]).astype(jnp.int32)

    x1 = swap(x0, "seq", 1)
    x2 = swap(x0, "seq", 2)

    few = rows // depth * wide
    w_rest, near, *pay = vmem_call(
        pack_kernel,
        [shape(depth, 3 * joined), shape(depth, 4 * joined + few)]
        + [shape(depth, joined + few)] * 3,
        scratch_shapes=[
            pltpu.VMEM((depth, 4 * wide), BF16),
            pltpu.VMEM((depth, 4 * narrow), BF16),
            pltpu.VMEM((depth, 4 * narrow), BF16),
            pltpu.VMEM((rows, 4 * wide), BF16),
            pltpu.SemaphoreType.DMA((4,)),
        ],
        smem=1,
        place=pltpu.HBM,
    )(place, w_query, w_key, value_weight, grad_attn[0])

    pay = [pay[0], swap(near, "seq", 1), swap(pay[1], "seq", 2), swap(pay[2], "seq", 3)]
    pay, x2 = lax.optimization_barrier((pay, x2))

    w_rows = jnp.stack([p[:, :joined] for p in pay])
    w_own = jnp.stack([w_rows] + [swap(w_rows, "fsdp", j) for j in (2, 4, 6)])
    u_rows = jnp.stack([w_rest, pay[1][:, joined : 4 * joined]])
    w_own, x1 = lax.optimization_barrier((w_own, x1))
    x3 = swap(x2, "seq", 1)
    x3, mark = lax.optimization_barrier((x3, note(8, x3)))
    w_other = swap(w_own, "fsdp", 1)
    u_part = [swap(u_rows, "fsdp", j) for j in (2, 4)]

    d = vmem_call(
        attend_kernel,
        [shape(2 * rows, joined + extra * (wide // 2)) for extra in (1, 2, 1)],
        scratch_shapes=[
            pltpu.VMEM((width, joined), BF16),
            pltpu.VMEM((4 * rows, wide), BF16),
            pltpu.VMEM((4 * rows, wide), BF16),
        ],
        smem=2,
        total=8 << 30,
    )(place, adjacency, x0, x1, x2, x3, w_own, w_other, *pay, mark)

    def weight_grad(parity, d):
        return vmem_call(
            functools.partial(weight_grad_kernel, parity),
            shape(4, 4, depth, joined, dtype=F32),
            smem=1,
            total=8 << 30,
        )(place, x0, x1, x2, x3, d[0], d[1])

    away = weight_grad(1, d)
    d, away, u_part = lax.optimization_barrier((d, away, u_part))
    sent = swap(away, "fsdp", 1)
    d_two = swap(d[2], "seq", 2)
    d_got = [d[0], swap(d[1], "seq", 1), d_two]
    onward = [d_got[1][:, :joined], d_got[1][:, joined + wide // 2 :]]
    onward = jnp.concatenate(onward, axis=1)
    d_got.append(swap(onward, "seq", 2))
    kept = weight_grad(0, d)
    total = kept + sent
    u_own = jnp.stack([u_rows, *u_part, swap(u_part[0], "fsdp", 4)])
    u_own, late = lax.optimization_barrier((u_own, total[0, 0, :8, :128]))
    u_other = swap(u_own, "fsdp", 1)
    got = [swap(total[i], "fsdp", 2 * i) for i in (1, 2, 3)]
    got, mark = lax.optimization_barrier((got, note(8, *got)))
    factor = 1.0 / math.sqrt(4 * rows * lax.axis_size("fsdp"))
    summed = (((total[0] + got[0]) + (got[1] + got[2])) * factor).astype(BF16)
    w_final = [summed[0]] + [swap(summed[j], "seq", j) for j in (1, 2, 3)]

    own, send = vmem_call(
        token_grad_kernel,
        [shape(rows, width // 2)] * 2,
        smem=1,
        total=6 << 30,
    )(place, *d_got, w_own, w_other, u_own, u_other, late)
    half = swap(send, "seq", 2)

    attended = vmem_call(
        attended_join_kernel, shape(rows, 4 * wide), smem=1
    )(place, *d_got)
    grad_wq, grad_wk, grad_wv, grad_in = vmem_call(
        join_kernel,
        [shape(depth, 4 * wide), shape(depth, 4 * narrow), shape(depth, 4 * narrow)]
        + [shape(rows, width)],
        smem=1,
    )(place, *w_final, mark, own, half)
    return attended[None], grad_in[None], grad_wq, grad_wk, grad_wv


def solution(mesh):
    by_heads = mesh.shape["seq"] == KEY_VALUE_HEADS and mesh.shape["fsdp"] == 8
    return jax.shard_map(
        head_body if by_heads else general_body,
        mesh=mesh,
        in_specs=(
            P("fsdp", "seq", None),
            P(),
            P(("fsdp", "seq"), None),
            P(("fsdp", "seq"), None),
            P(("fsdp", "seq"), None),
            P("fsdp", "seq", None),
        ),
        out_specs=(
            P("fsdp", "seq", None),
            P("fsdp", "seq", None),
            P(("fsdp", "seq"), None),
            P(("fsdp", "seq"), None),
            P(("fsdp", "seq"), None),
        ),
        check_vma=False,
    )
```
